512 devices in a mesh: slab: 16 (over z, core), tile: 32 (over x, y).
Axes of the slice: x: 4, y: 8, z: 8, core: 2. Of those that a mesh axis runs over, the one named last changes fastest.
Arguments:
- density: bfloat16 [262144, 512], P(('slab', 'tile')), may hold values from 0.049804688 to 4
- brick_color: float32 [3, 262144], P(None, ('slab', 'tile')), may hold values from 0.1 to 1
- brick_row: int32 [262144], P(('slab', 'tile')), may hold values from 0 to 31, as said below
- brick_col: int32 [262144], P(('slab', 'tile')), may hold values from 0 to 1023, as said below
- brick_steps: int32 [262144], P(('slab', 'tile')), may hold values from 1 to 8
- depth_flip: int32 [32, 1024], P(None, 'tile'), may hold values from 0 to 1
- w_in: bfloat16 [32, 4, 3, 3], replicated, may hold values from -1.5 to 1.5
- w_enc: bfloat16 [32, 32, 3, 3], replicated, may hold values from -0.5 to 0.5
- w_dec: bfloat16 [32, 32, 3, 3], replicated, may hold values from -0.5 to 0.5
- w_dec2: bfloat16 [32, 32, 3, 3], replicated, may hold values from -0.5 to 0.5
- w_out: bfloat16 [3, 32], replicated, may hold values from -1 to 1
Outputs:
- denoised: bfloat16 [3, 256, 8192], P(None, 'slab', 'tile')
The draws below stay inside these ranges and needn't reach their ends.
Inputs may be any that keep to these rules, and one draw needn't show every extreme that they name: `brick_row`: within one slab no two bricks name the same screen tile. The bricks of one device name at most 32 tiles in any one column block (tile columns j * 32 to (j + 1) * 32 - 1); in every slab some column block gets exactly 32 bricks from every device of that slab. `brick_col`: see brick_row.
All inputs are finite; a program needn't handle non-finite values.
Results may differ from the reference program's by a relative error of at most 0.0086.
Values may be sent and summed in bfloat16 or wider, within the bound.
A program may use at most 64 MiB of HBM per device.

```python
import math
import jax
import jax.numpy as jnp
from jax import lax

PW = 256
CHANNELS = 32
VOXELS = 512
H = 256
W = 8192
TH = 32
TW = 1024
TILES_OWN = 1024
CAP = 32
BRICK_DEV = 512
BRICKS = 262144
N_SLAB = 16
N_TILE = 32


def brick_layout(key):
    slots = N_TILE * CAP
    tile_cols = PW // 8
    devices = N_SLAB * N_TILE
    hot_key, pick_key, mix_key, place_key = jax.random.split(key, 4)
    hottest = jax.random.randint(hot_key, (N_SLAB,), 0, N_TILE)
    hot_dev = jnp.repeat(hottest, N_TILE)
    orders = jax.vmap(lambda sub: jax.random.permutation(sub, slots))(jax.random.split(pick_key, devices))
    position = jnp.argsort(orders, axis=1, stable=True).astype(jnp.int32)
    slot_ids = jnp.arange(slots, dtype=jnp.int32)[None, :]
    is_hot = slot_ids // CAP == hot_dev[:, None]
    priority = jnp.where(is_hot, slot_ids - slots, position)
    chosen = jnp.argsort(priority, axis=1, stable=True)[:, :BRICK_DEV].astype(jnp.int32)
    mixing = jax.vmap(lambda sub: jax.random.permutation(sub, BRICK_DEV))(jax.random.split(mix_key, devices))
    chosen = jnp.take_along_axis(chosen, mixing.astype(jnp.int32), axis=1)
    owners = chosen // CAP
    ranks = chosen % CAP
    dev_ids = jnp.arange(devices, dtype=jnp.int32)[:, None]
    slab_ids = dev_ids // N_TILE
    source = dev_ids % N_TILE
    places = jax.vmap(lambda sub: jax.random.permutation(sub, TILES_OWN))(jax.random.split(place_key, devices)).astype(jnp.int32)
    flat_places = places.reshape(-1)
    local = flat_places[(slab_ids * N_TILE + owners) * TILES_OWN + source * CAP + ranks]
    rows = local // tile_cols
    cols = owners * tile_cols + local % tile_cols
    return (rows.reshape(-1).astype(jnp.int32), cols.reshape(-1).astype(jnp.int32))


def draw_brick_row(key, part):
    layout = brick_layout(key)
    return layout[0]


def draw_brick_col(key, part):
    layout = brick_layout(key)
    return layout[1]


def with_ends(values, key, low, top_value):
    longest = values.shape.index(max(values.shape))
    spots = []
    for shift in (0, 1):
        where = [jax.random.randint(jax.random.fold_in(key, axis), (), 0, length) for axis, length in enumerate(values.shape)]
        where[longest] = (where[longest] + shift) % values.shape[longest]
        spots.append(tuple(where))
    return values.at[spots[0]].set(low).at[spots[1]].set(top_value)


def steps_of(own_key, extent, pieces, low, largest):
    def one(dim, blocks):
        heights = jax.random.uniform(jax.random.fold_in(jax.random.fold_in(own_key, 6), dim), (blocks,), jnp.float32, low / len(pieces), largest / len(pieces))
        return jnp.repeat(jnp.exp(heights), extent[dim] // blocks).reshape((-1,) + (1,) * (len(extent) - dim - 1))

    gain = one(*pieces[0])
    for cut in pieces[1:]:
        gain = gain * one(*cut)
    return gain


def gaussian(rng, extent, spread, limit, held_as=jnp.bfloat16):
    drawn = jax.random.normal(rng, extent, jnp.float32) * spread
    return jnp.minimum(jnp.maximum(drawn, -limit), limit).astype(held_as)


def setup_inputs(seed: int = 0) -> dict:
    key_of = jax.random.split(jax.random.key(seed), 12)
    return {
        "density": jnp.clip(jnp.exp(math.log(4.0) - 4.3859405 * jax.random.uniform(key_of[0], (BRICKS, VOXELS), jnp.float32) ** steps_of(key_of[0], (BRICKS, VOXELS), ((0, 512),), -0.2, 0.2)), 0.049804688, 4.0).astype(jnp.bfloat16),
        "brick_color": jnp.clip(0.1 + 0.9 * jax.random.uniform(key_of[1], (3, BRICKS), jnp.float32) ** steps_of(key_of[1], (3, BRICKS), ((1, 512),), -0.2, 0.2), 0.1, 1.0),
        "brick_row": draw_brick_row(jax.random.fold_in(key_of[11], 71), 0),
        "brick_col": draw_brick_col(jax.random.fold_in(key_of[11], 71), 0),
        "brick_steps": with_ends(jax.random.randint(key_of[4], (BRICKS,), 1, 9), jax.random.fold_in(key_of[4], 1), 1, 8).astype(jnp.int32),
        "depth_flip": with_ends(jax.random.randint(key_of[5], (TH, TW), 0, 2), jax.random.fold_in(key_of[5], 1), 0, 1).astype(jnp.int32),
        "w_in": gaussian(key_of[6], (CHANNELS, 4, 3, 3), 18 ** -0.5, 1.5),
        "w_enc": gaussian(key_of[7], (CHANNELS, CHANNELS, 3, 3), 144 ** -0.5, 0.5),
        "w_dec": gaussian(key_of[8], (CHANNELS, CHANNELS, 3, 3), 144 ** -0.5, 0.5),
        "w_dec2": gaussian(key_of[9], (CHANNELS, CHANNELS, 3, 3), 144 ** -0.5, 0.5),
        "w_out": gaussian(key_of[10], (3, CHANNELS), CHANNELS ** -0.5, 1.0),
    }


STEP = 0.03


def ray_march(density, brick_color, brick_steps):
    count = density.shape[0]
    sigmas = density.astype(jnp.float32).reshape(count, 8, 64)
    tint = jnp.transpose(brick_color).astype(jnp.float32)[:, :, None]
    trans = jnp.ones((count, 64), jnp.float32)
    light = jnp.zeros((count, 3, 64), jnp.float32)
    for depth_idx in range(8):
        sigma = sigmas[:, depth_idx, :]
        alive = (brick_steps > depth_idx)[:, None]
        opacity = jnp.where(alive, 1.0 - jnp.exp(-STEP * sigma), 0.0)
        light = light + (trans * opacity * sigma)[:, None, :] * tint
        trans = trans * (1.0 - opacity)
    joined = jnp.concatenate([light, (1.0 - trans)[:, None, :]], axis=1)
    return joined.reshape(count, 256).astype(jnp.bfloat16)


def convolve(field, kernel):
    return lax.conv_general_dilated(field[None], kernel, (1, 1), "VALID", dimension_numbers=("NCHW", "OIHW", "NCHW"), preferred_element_type=jnp.float32)[0]


def padded(field):
    return jnp.pad(field, ((0, 0), (1, 1), (1, 1)))


def reference(density, brick_color, brick_row, brick_col, brick_steps, depth_flip, w_in, w_enc, w_dec, w_dec2, w_out):
    per_slab = BRICK_DEV * N_TILE

    def render(slab_idx):
        start = (slab_idx * per_slab).astype(jnp.int32)
        dens_block = lax.dynamic_slice_in_dim(density, start, per_slab, 0)
        tint_block = lax.dynamic_slice_in_dim(brick_color, start, per_slab, 1)
        step_block = lax.dynamic_slice_in_dim(brick_steps, start, per_slab, 0)
        row_block = lax.dynamic_slice_in_dim(brick_row, start, per_slab, 0)
        col_block = lax.dynamic_slice_in_dim(brick_col, start, per_slab, 0)
        partials = ray_march(dens_block, tint_block, step_block)
        canvas = jnp.zeros((TH * TW, 256), jnp.bfloat16)
        return canvas.at[(row_block * TW + col_block).astype(jnp.int32)].set(partials)

    canvases = lax.map(render, jnp.arange(N_SLAB, dtype=jnp.int32))
    flipped = (depth_flip.reshape(TH * TW) == 1)[:, None]
    light = jnp.zeros((TH * TW, 192), jnp.float32)
    trans = jnp.ones((TH * TW, 64), jnp.float32)
    for layer_idx in range(N_SLAB):
        piece = jnp.where(flipped, canvases[N_SLAB - 1 - layer_idx], canvases[layer_idx]).astype(jnp.float32)
        light = light + jnp.tile(trans, (1, 3)) * piece[:, :192]
        trans = trans * (1.0 - piece[:, 192:])
    tiles = jnp.concatenate([light, 1.0 - trans], axis=1).astype(jnp.bfloat16)
    composite = jnp.transpose(tiles.reshape(TH, TW, 4, 8, 8), (2, 0, 3, 1, 4)).reshape(4, H, W)
    e_first = jax.nn.relu(convolve(padded(composite), w_in)).astype(jnp.bfloat16)
    e_second = jax.nn.relu(convolve(padded(e_first), w_enc)).astype(jnp.bfloat16)
    d_first = jax.nn.relu(convolve(padded(e_second), w_dec)).astype(jnp.bfloat16)
    d_second = jax.nn.relu(convolve(padded(d_first), w_dec2) + e_first.astype(jnp.float32)).astype(jnp.bfloat16)
    projected = jnp.dot(w_out, d_second.reshape(CHANNELS, H * W), preferred_element_type=jnp.float32).reshape(3, H, W)
    return (composite[:3].astype(jnp.float32) + projected).astype(jnp.bfloat16)
```

```python
import functools
import jax
import jax.numpy as jnp
from jax import lax
from jax.experimental import pallas as pl
from jax.experimental.pallas import tpu as pltpu
from jax.sharding import PartitionSpec as P

MESH = pl.DeviceIdType.MESH
BF16 = jnp.bfloat16
F32 = jnp.float32
STEP = 0.03
CAP = 32
PITCH = 40
PAD = 8
LIGHT_TOP = 2.5
ALPHA_TOP = 0.625
LEVELS = 65535.0


def iota(shape, dim):
    return lax.broadcasted_iota(jnp.int32, shape, dim)


def as_bf16(cond):
    return jnp.where(cond, 1.0, 0.0).astype(BF16)


def mm(a, b):
    return jnp.dot(a, b, preferred_element_type=F32)


def mm_nt(a, b):
    return lax.dot_general(a, b, (((1,), (1,)), ((), ())), preferred_element_type=F32)


def mm_tn(a, b):
    return lax.dot_general(a, b, (((0,), (0,)), ((), ())), preferred_element_type=F32)


def scales(shape):
    front = iota(shape, 1) < 64
    return jnp.where(front, LIGHT_TOP / LEVELS, ALPHA_TOP / LEVELS)


def split(levels):
    high = levels // 256
    low = levels - 256 * high
    return jnp.concatenate([high.astype(F32), low.astype(F32)], axis=1).astype(BF16)


def join(halves):
    levels = (256.0 * halves[:, 0:128] + halves[:, 128:256]).astype(jnp.int32)
    return (levels - 32768).astype(jnp.int16)


def build_weights(w_in, w_layers, w_out, w1, wb, wo):
    spread = as_bf16(iota((32, 256), 0) == iota((32, 256), 1) % 32)
    lane_x = iota((32, 256), 1) // 32
    for layer, w_ref in enumerate(w_layers):
        turned = jnp.transpose(w_ref[...].astype(F32))
        for ky in range(3):
            taps = [
                mm(turned[:, 32 * (3 * ky + kx) : 32 * (3 * ky + kx) + 32].astype(BF16), spread)
                for kx in range(3)
            ]
            base = 256 * ky
            for x_in in range(8):
                total = jnp.zeros((32, 256), F32)
                for kx in range(3):
                    total = jnp.where(lane_x == x_in - kx + 1, taps[kx], total)
                wb[layer, base + 32 * x_in : base + 32 * x_in + 32, :] = total.astype(BF16)
            edge = 768 + 128 * ky
            wb[layer, edge : edge + 32, :] = jnp.where(lane_x == 7, taps[2], 0.0).astype(BF16)
            wb[layer, edge + 32 : edge + 96, :] = jnp.zeros((64, 256), BF16)
            wb[layer, edge + 96 : edge + 128, :] = jnp.where(lane_x == 0, taps[0], 0.0).astype(BF16)
    row = iota((128, 256), 0)
    lane_x = iota((128, 256), 1) // 32
    third = row // 32
    x_in = (row % 32) // 4 + jnp.where(third == 1, -8, jnp.where(third == 2, 8, 0))
    pick = as_bf16((iota((128, 4), 0) % 4 == iota((128, 4), 1)) & (iota((128, 4), 0) < 96))
    for ky in range(3):
        total = jnp.zeros((128, 256), F32)
        for kx in range(3):
            tap = mm(mm(pick, w_in[3 * ky + kx]).astype(BF16), spread)
            total = jnp.where(lane_x == x_in - kx + 1, tap, total)
        w1[128 * ky : 128 * ky + 128, :] = total.astype(BF16)
    spread_t = as_bf16(iota((256, 32), 1) == iota((256, 32), 0) % 32)
    same_x = iota((256, 256), 0) // 32 == iota((256, 256), 1) % 8
    row = iota((128, 256), 0)
    for c in range(3):
        along = mm_nt(spread_t, jnp.broadcast_to(w_out[c : c + 1, :], (256, 32)))
        wo[0:256, 256 * c : 256 * c + 256] = jnp.where(same_x, along, 0.0).astype(BF16)
        own = (row < 32) & (row % 4 == c) & (row // 4 == iota((128, 256), 1) % 8)
        wo[256:384, 256 * c : 256 * c + 256] = as_bf16(own)


def ray_march(density, steps, part):
    lane = iota((64, 128), 1)
    front = lane < 64
    half = jnp.where(front, 0, 1)
    for chunk in range(density.shape[0] // 64):
        rows = slice(64 * chunk, 64 * chunk + 64)
        group = steps[:, 128 * (64 * chunk // 128) : 128 * (64 * chunk // 128) + 128].astype(F32)
        off = (64 * chunk) % 128
        eye = iota((64, 128), 0) + off == iota((64, 128), 1)
        alive = mm(jnp.where(eye, group, 0.0).astype(BF16), jnp.ones((128, 128), BF16))
        alive = alive.astype(jnp.int32)
        light = jnp.zeros((64, 128), F32)
        trans = jnp.ones((64, 128), F32)
        for j in range(4):
            sigma = density[rows, 128 * j : 128 * j + 128].astype(F32)
            keep = jnp.where(half + 2 * j < alive, jnp.exp(-STEP * sigma), 1.0)
            emit = (1.0 - keep) * sigma
            other = pltpu.roll(keep, 64, 1)
            light = light + trans * jnp.where(front, 1.0, other) * emit
            trans = trans * (keep * other)
        light = light + pltpu.roll(light, 64, 1)
        value = jnp.where(
            front, light * (LEVELS / LIGHT_TOP), (1.0 - trans) * (LEVELS / ALPHA_TOP)
        )
        part[rows, :] = split((value + 0.5).astype(jnp.int32))


def kernel(
    n_slab,
    n_tile,
    density,
    color,
    brick_row,
    brick_col,
    steps,
    flip,
    w_in,
    w_enc,
    w_dec,
    w_dec2,
    w_out,
    out,
    part,
    place,
    canvas_of,
    a_out,
    a_in,
    am_out,
    am_in,
    canvas,
    b_out,
    b_in,
    bm_out,
    bm_in,
    tint,
    h_own,
    h_edge,
    h_rows,
    h_sides,
    ext,
    x0,
    x1,
    e1,
    e2,
    d1,
    edge,
    w1,
    wb,
    wo,
    am_send,
    am_recv,
    a_send,
    a_recv,
    bm_send,
    bm_recv,
    b_send,
    b_recv,
    h_send,
    h_recv,
):
    s = lax.axis_index("slab")
    t = lax.axis_index("tile")
    bricks = density.shape[0]
    slots = CAP * n_tile
    owned = 64 * n_slab

    def tile_peer(i):
        return (s, lax.rem(t + i, n_tile))

    def slab_peer(j):
        return (lax.rem(s + j, n_slab), t)

    def near(ds, dt):
        return (lax.rem(s + ds + n_slab, n_slab), lax.rem(t + dt + n_tile, n_tile))

    corners = [near(-1, -1), near(-1, 1), near(1, -1), near(1, 1)]
    greeted = (
        [tile_peer(i) for i in range(1, n_tile)]
        + [slab_peer(j) for j in range(1, n_slab)]
        + corners
    )
    barrier = pltpu.get_barrier_semaphore()
    for peer in greeted:
        pl.semaphore_signal(barrier, inc=1, device_id=peer, device_id_type=MESH)

    col = brick_col[...]
    row = brick_row[...]
    rel = (col // 32 - t + n_tile) % n_tile
    mine = iota((n_tile, bricks), 0) == rel
    before = as_bf16(iota((bricks, bricks), 0) < iota((bricks, bricks), 1))
    ahead = mm(as_bf16(mine), before)
    rank = jnp.sum(jnp.where(mine, ahead, 0.0), axis=0, keepdims=True).astype(jnp.int32)
    slot = rel * CAP + rank
    place[...] = as_bf16(iota((slots, bricks), 0) == slot)
    block = (row // 2 - s + n_slab) % n_slab
    tile_hi = (block * 2 + row % 2 + 1).astype(F32)
    tile_lo = (col % 32).astype(F32)
    tints = color[...]
    tints_hi = tints.astype(BF16).astype(F32)
    tints_lo = tints - tints_hi
    field = iota((16, bricks), 0)
    meta = jnp.zeros((16, bricks), F32)
    for c in range(3):
        meta = jnp.where(field == 2 * c, tints_hi[c : c + 1, :], meta)
        meta = jnp.where(field == 2 * c + 1, tints_lo[c : c + 1, :], meta)
    meta = jnp.where(field == 6, tile_hi, meta)
    meta = jnp.where(field == 7, tile_lo, meta)
    meta = jnp.where(field == 8, 1.0, meta)
    sent_meta = mm_nt(meta.astype(BF16), place[...]).astype(BF16)
    for g in range(slots // 128):
        am_out[g] = sent_meta[:, 128 * g : 128 * g + 128]
    am_in[0] = am_out[0]

    pl.semaphore_wait(barrier, len(greeted))

    def start(src, dst, send, recv, peer):
        copy = pltpu.make_async_remote_copy(
            src_ref=src,
            dst_ref=dst,
            send_sem=send,
            recv_sem=recv,
            device_id=peer,
            device_id_type=MESH,
        )
        copy.start()
        return copy

    am_copies = [
        start(am_out.at[i // 4], am_in.at[i], am_send.at[i], am_recv.at[i], tile_peer(i))
        for i in range(1, n_tile)
    ]

    ray_march(density, steps, part)
    a_copies = []
    for g in range(slots // 128):
        a_out[128 * g : 128 * g + 128, :] = join(
            mm(place[128 * g : 128 * g + 128, :], part[...])
        )
        for i in range(4 * g, 4 * g + 4):
            span = pl.ds(CAP * i, CAP)
            if i == 0:
                a_in[0:CAP, :] = a_out[0:CAP, :]
            else:
                a_copies.append(
                    start(
                        a_out.at[span], a_in.at[span], a_send.at[i], a_recv.at[i], tile_peer(i)
                    )
                )

    for copy in am_copies:
        copy.wait_recv()
    lane = iota((16, 128), 1)
    groups = []
    for g in range(slots // 128):
        got = am_in[4 * g].astype(F32)
        for q in range(1, 4):
            got = jnp.where(lane // 32 == q, am_in[4 * g + q].astype(F32), got)
        groups.append(got)
    arrived = jnp.concatenate(groups, axis=1)
    tile_id = (32.0 * arrived[6:7, :] + arrived[7:8, :] - 32.0).astype(jnp.int32)
    canvas_of[...] = as_bf16(iota((owned, slots), 0) == tile_id)
    tile_meta = mm_nt(arrived.astype(BF16), canvas_of[...]).astype(BF16)
    for g in range(n_slab // 2):
        bm_out[g] = tile_meta[:, 128 * g : 128 * g + 128]
    bm_in[0] = bm_out[0]
    bm_copies = [
        start(bm_out.at[j // 2], bm_in.at[j], bm_send.at[j], bm_recv.at[j], slab_peer(j))
        for j in range(1, n_slab)
    ]

    build_weights(w_in, (w_enc, w_dec, w_dec2), w_out, w1, wb, wo)
    ext[...] = jnp.zeros(ext.shape, F32)
    for ref in (x0, e1, e2, d1):
        width = ref.shape[1]
        ref[0:PAD, :] = jnp.zeros((PAD, width), F32)
        ref[ref.shape[0] - PAD :, :] = jnp.zeros((PAD, width), F32)

    chunk = min(256, slots)
    for k in range(slots // chunk):
        for i in range(max(1, k * chunk // CAP), (k + 1) * chunk // CAP):
            a_copies[i - 1].wait_recv()
        span = slice(k * chunk, (k + 1) * chunk)
        term = mm(canvas_of[:, span], split(a_in[span, :].astype(jnp.int32) + 32768))
        if k == 0:
            canvas[...] = term
        else:
            canvas[...] += term
    b_copies = []
    for j in range(n_slab):
        piece = join(canvas[64 * j : 64 * j + 64, :])
        if j == 0:
            b_in[0] = piece
        else:
            b_out[j] = piece
            b_copies.append(
                start(b_out.at[j], b_in.at[j], b_send.at[j], b_recv.at[j], slab_peer(j))
            )

    for copy in bm_copies:
        copy.wait_recv()
    lane_c = iota((16, 256), 1) // 64
    field = iota((16, 256), 0)
    choose = as_bf16(((field // 2 == lane_c) & (lane_c < 3) & (field < 6)) | ((field == 8) & (lane_c == 3)))
    for j in range(n_slab):
        both = mm_tn(bm_in[j], choose)
        tint[j] = both[64 * (j % 2) : 64 * (j % 2) + 64, :]

    flips = flip[pl.ds(2 * s, 2), :]
    same = iota((32, 32), 0) == iota((32, 32), 1)
    flipped = (
        jnp.concatenate(
            [
                jnp.sum(jnp.where(same, flips[r : r + 1, :], 0), axis=1, keepdims=True)
                for r in range(2)
            ],
            axis=0,
        )
        == 1
    )

    for copy in b_copies:
        copy.wait_recv()
    front = iota((64, 128), 1) < 64
    scale = scales((64, 128))
    light0 = jnp.zeros((64, 128), F32)
    light1 = jnp.zeros((64, 128), F32)
    trans = jnp.ones((64, 128), F32)
    for k in range(n_slab):
        first = lax.rem(s - k + n_slab, n_slab)
        last = lax.rem(s - (n_slab - 1 - k) + n_slab, n_slab)
        level = jnp.where(
            flipped, b_in[last].astype(jnp.int32), b_in[first].astype(jnp.int32)
        )
        piece = (level + 32768).astype(F32) * scale
        hue = jnp.where(flipped, tint[last], tint[first])
        turned = pltpu.roll(piece, 64, 1)
        part0 = (jnp.where(front, piece, turned) * hue[:, 0:128]).astype(BF16).astype(F32)
        part1 = (piece * hue[:, 128:256]).astype(BF16).astype(F32)
        alpha = jnp.where(front, pltpu.roll(part1, 64, 1), part1)
        light0 = light0 + trans * part0
        light1 = light1 + trans * part1
        trans = trans * (1.0 - alpha)
    composite = jnp.concatenate([light0, light1], axis=1).astype(BF16)
    h_own[...] = composite
    own = composite.astype(F32)
    edge_row = iota((16, 256), 0)
    for side, at in ((0, 0), (1, 31)):
        h_edge[side] = jnp.where(
            edge_row == 0,
            own[at : at + 1, :],
            jnp.where(edge_row == 1, own[at + 32 : at + 33, :], 0.0),
        ).astype(BF16)
    up, down, left, right = near(-1, 0), near(1, 0), near(0, -1), near(0, 1)
    plan = [
        (h_own.at[pl.ds(0, 32)], h_rows.at[1], up),
        (h_own.at[pl.ds(32, 32)], h_rows.at[0], down),
        (h_edge.at[0], h_sides.at[1], left),
        (h_edge.at[1], h_sides.at[0], right),
        (h_edge.at[0], h_sides.at[5], corners[0]),
        (h_edge.at[1], h_sides.at[4], corners[1]),
        (h_edge.at[0], h_sides.at[3], corners[2]),
        (h_edge.at[1], h_sides.at[2], corners[3]),
    ]
    h_copies = [
        start(src, dst, h_send.at[n], h_recv.at[n], peer) for n, (src, dst, peer) in enumerate(plan)
    ]
    has_up = jnp.where(s > 0, 1.0, 0.0)
    has_down = jnp.where(s < n_slab - 1, 1.0, 0.0)
    has_left = jnp.where(t > 0, 1.0, 0.0)
    has_right = jnp.where(t < n_tile - 1, 1.0, 0.0)
    ext[PITCH + 1 : PITCH + 33, :] = own[0:32, :]
    ext[2 * PITCH + 1 : 2 * PITCH + 33, :] = own[32:64, :]
    for copy in h_copies:
        copy.wait_recv()
    ext[1:33, :] = h_rows[0].astype(F32) * has_up
    ext[3 * PITCH + 1 : 3 * PITCH + 33, :] = h_rows[1].astype(F32) * has_down
    sides = [
        (0, has_left, ((PITCH, 0), (2 * PITCH, 1))),
        (1, has_right, ((PITCH + 33, 0), (2 * PITCH + 33, 1))),
        (2, has_up * has_left, ((0, 1),)),
        (3, has_up * has_right, ((33, 1),)),
        (4, has_down * has_left, ((3 * PITCH, 0),)),
        (5, has_down * has_right, ((3 * PITCH + 33, 0),)),
    ]
    for n, there, moves in sides:
        block = h_sides[n].astype(F32) * there
        for at, r in moves:
            ext[at : at + 1, :] = block[r : r + 1, :]

    tiles = ext[...].astype(BF16)
    lane = iota((256, 128), 1)
    source = (lane % 4) * 64 + (lane % 32) // 4
    for y in range(8):
        turn = as_bf16((iota((256, 128), 0) == source + 8 * y) & (lane < 96))
        rows = mm(tiles, turn)
        for tr in range(4):
            r = 8 * tr + y - 4
            if 0 <= r < 24:
                x0[PAD + PITCH * r : PAD + PITCH * r + PITCH, :] = rows[
                    PITCH * tr : PITCH * tr + PITCH, :
                ]
    n = 24 * PITCH
    lane = iota((n, 128), 1)
    x1[...] = jnp.where(
        lane < 32, x0[PAD : PAD + n, :], jnp.where(lane < 64, x0[PAD - 1 : PAD - 1 + n, :], x0[PAD + 1 : PAD + 1 + n, :])
    )

    group = iota((PITCH, 256), 0)
    inside = jnp.where(
        group == 0, has_left, jnp.where(group >= 33, has_right, 1.0)
    )[None]

    def finish(ref, value, outer):
        rows = value.shape[0] // PITCH
        kept = jnp.maximum(value, 0.0).reshape(rows, PITCH, 256) * inside
        ref[PAD : PAD + rows * PITCH, :] = (
            kept.reshape(rows * PITCH, 256).astype(BF16).astype(F32)
        )

        @pl.when(s == 0)
        def _():
            ref[PAD : PAD + outer * PITCH, :] = jnp.zeros((outer * PITCH, 256), F32)

        @pl.when(s == n_slab - 1)
        def _():
            ref[PAD + (rows - outer) * PITCH : PAD + rows * PITCH, :] = jnp.zeros(
                (outer * PITCH, 256), F32
            )

    m = 22 * PITCH
    wide = jnp.concatenate(
        [x1[PITCH * dy : PITCH * dy + m, :].astype(BF16) for dy in range(3)], axis=1
    )
    finish(e1, mm(wide, w1[...]), 3)

    def convolve(ref, layer, rows_in):
        n = rows_in * PITCH
        m = (rows_in - 2) * PITCH
        lane = iota((n, 128), 1)
        edge[0:n, :] = jnp.where(
            lane < 32,
            ref[PAD + 1 : PAD + 1 + n, 0:128],
            jnp.where(lane >= 96, ref[PAD - 1 : PAD - 1 + n, 128:256], 0.0),
        )
        wide = jnp.concatenate(
            [ref[PAD + PITCH * dy : PAD + PITCH * dy + m, :].astype(BF16) for dy in range(3)]
            + [edge[PITCH * dy : PITCH * dy + m, :].astype(BF16) for dy in range(3)],
            axis=1,
        )
        return mm(wide, wb[layer])

    finish(e2, convolve(e1, 0, 22), 2)
    finish(d1, convolve(e2, 1, 20), 1)
    m = 16 * PITCH
    d2 = jnp.maximum(convolve(d1, 2, 18) + e1[PAD + 3 * PITCH : PAD + 3 * PITCH + m, :], 0.0)
    last = jnp.concatenate(
        [d2.astype(BF16), x0[PAD + 4 * PITCH : PAD + 4 * PITCH + m, :].astype(BF16)], axis=1
    )
    own_group = (iota((PITCH, 256), 0) - 1 == iota((PITCH, 256), 1) // 8)[None]
    first_of = iota((16, m), 0) * PITCH
    of_row = as_bf16((iota((16, m), 1) >= first_of) & (iota((16, m), 1) < first_of + PITCH))
    for c in range(3):
        color_c = mm(last, wo[:, 256 * c : 256 * c + 256]).reshape(16, PITCH, 256)
        color_c = jnp.where(own_group, color_c, 0.0).reshape(m, 256).astype(BF16)
        out[c] = mm(of_row, color_c).astype(BF16)

    for copy in am_copies + a_copies + bm_copies + b_copies + h_copies:
        copy.wait_send()


def shards(
    density,
    brick_color,
    brick_row,
    brick_col,
    brick_steps,
    depth_flip,
    w_in,
    w_enc,
    w_dec,
    w_dec2,
    w_out,
):
    n_tile = lax.axis_size("tile")
    n_slab = lax.axis_size("slab")
    bricks = density.shape[0]
    slots = CAP * n_tile
    owned = 64 * n_slab
    taps = [jnp.transpose(w, (2, 3, 0, 1)).reshape(288, 32) for w in (w_enc, w_dec, w_dec2)]
    vmem = pl.BlockSpec(memory_space=pltpu.VMEM)
    dma = pltpu.SemaphoreType.DMA
    return pl.pallas_call(
        functools.partial(kernel, n_slab, n_tile),
        out_shape=jax.ShapeDtypeStruct((3, 16, 256), BF16),
        in_specs=[vmem] * 11,
        out_specs=vmem,
        scratch_shapes=[
            pltpu.VMEM((bricks, 256), BF16),
            pltpu.VMEM((slots, bricks), BF16),
            pltpu.VMEM((owned, slots), BF16),
            pltpu.VMEM((slots, 128), jnp.int16),
            pltpu.VMEM((slots, 128), jnp.int16),
            pltpu.VMEM((slots // 128, 16, 128), BF16),
            pltpu.VMEM((n_tile, 16, 128), BF16),
            pltpu.VMEM((owned, 256), F32),
            pltpu.VMEM((n_slab, 64, 128), jnp.int16),
            pltpu.VMEM((n_slab, 64, 128), jnp.int16),
            pltpu.VMEM((n_slab // 2, 16, 128), BF16),
            pltpu.VMEM((n_slab, 16, 128), BF16),
            pltpu.VMEM((n_slab, 64, 256), F32),
            pltpu.VMEM((64, 256), BF16),
            pltpu.VMEM((2, 16, 256), BF16),
            pltpu.VMEM((2, 32, 256), BF16),
            pltpu.VMEM((6, 16, 256), BF16),
            pltpu.VMEM((4 * PITCH, 256), F32),
            pltpu.VMEM((24 * PITCH + 2 * PAD, 128), F32),
            pltpu.VMEM((24 * PITCH, 128), F32),
            pltpu.VMEM((22 * PITCH + 2 * PAD, 256), F32),
            pltpu.VMEM((20 * PITCH + 2 * PAD, 256), F32),
            pltpu.VMEM((18 * PITCH + 2 * PAD, 256), F32),
            pltpu.VMEM((22 * PITCH, 128), F32),
            pltpu.VMEM((384, 256), BF16),
            pltpu.VMEM((3, 1152, 256), BF16),
            pltpu.VMEM((384, 768), BF16),
            dma((n_tile,)),
            dma((n_tile,)),
            dma((n_tile,)),
            dma((n_tile,)),
            dma((n_slab,)),
            dma((n_slab,)),
            dma((n_slab,)),
            dma((n_slab,)),
            dma((8,)),
            dma((8,)),
        ],
        compiler_params=pltpu.CompilerParams(
            collective_id=0, has_side_effects=True, vmem_limit_bytes=48 * 1024 * 1024
        ),
    )(
        density,
        brick_color,
        brick_row.reshape(1, bricks),
        brick_col.reshape(1, bricks),
        brick_steps.reshape(1, bricks),
        depth_flip,
        jnp.transpose(w_in, (2, 3, 1, 0)).reshape(9, 4, 32),
        *taps,
        w_out,
    )


def solution(mesh):
    return jax.shard_map(
        shards,
        mesh=mesh,
        in_specs=(
            P(("slab", "tile"), None),
            P(None, ("slab", "tile")),
            P(("slab", "tile")),
            P(("slab", "tile")),
            P(("slab", "tile")),
            P(None, "tile"),
            P(),
            P(),
            P(),
            P(),
            P(),
        ),
        out_specs=P(None, "slab", "tile"),
        check_vma=False,
    )
```

```python
import functools
import jax
import jax.numpy as jnp
from jax import lax
from jax.experimental import pallas as pl
from jax.experimental.pallas import tpu as pltpu
from jax.sharding import PartitionSpec as P

MESH = pl.DeviceIdType.MESH
BF16 = jnp.bfloat16
F32 = jnp.float32
STEP = 0.03
CAP = 32
PITCH = 40
PAD = 8
LIGHT_TOP = 2.5
ALPHA_TOP = 0.625
LEVELS = 65535.0


def iota(shape, dim):
    return lax.broadcasted_iota(jnp.int32, shape, dim)


def as_bf16(cond):
    return jnp.where(cond, 1.0, 0.0).astype(BF16)


def mm(a, b):
    return jnp.dot(a, b, preferred_element_type=F32)


def mm_nt(a, b):
    return lax.dot_general(a, b, (((1,), (1,)), ((), ())), preferred_element_type=F32)


def mm_tn(a, b):
    return lax.dot_general(a, b, (((0,), (0,)), ((), ())), preferred_element_type=F32)


def scales(shape):
    front = iota(shape, 1) < 64
    return jnp.where(front, LIGHT_TOP / LEVELS, ALPHA_TOP / LEVELS)


def split(levels):
    high = levels // 256
    low = levels - 256 * high
    return jnp.concatenate([high.astype(F32), low.astype(F32)], axis=1).astype(BF16)


def join(halves):
    levels = (256.0 * halves[:, 0:128] + halves[:, 128:256]).astype(jnp.int32)
    return (levels - 32768).astype(jnp.int16)


def build_weights(w_in, w_layers, w_out, w1, wb, wo):
    spread = as_bf16(iota((32, 256), 0) == iota((32, 256), 1) % 32)
    lane_x = iota((32, 256), 1) // 32
    for layer, w_ref in enumerate(w_layers):
        turned = jnp.transpose(w_ref[...].astype(F32))
        for ky in range(3):
            taps = [
                mm(turned[:, 32 * (3 * ky + kx) : 32 * (3 * ky + kx) + 32].astype(BF16), spread)
                for kx in range(3)
            ]
            base = 256 * ky
            for x_in in range(8):
                total = jnp.zeros((32, 256), F32)
                for kx in range(3):
                    total = jnp.where(lane_x == x_in - kx + 1, taps[kx], total)
                wb[layer, base + 32 * x_in : base + 32 * x_in + 32, :] = total.astype(BF16)
            edge = 768 + 128 * ky
            wb[layer, edge : edge + 32, :] = jnp.where(lane_x == 7, taps[2], 0.0).astype(BF16)
            wb[layer, edge + 32 : edge + 96, :] = jnp.zeros((64, 256), BF16)
            wb[layer, edge + 96 : edge + 128, :] = jnp.where(lane_x == 0, taps[0], 0.0).astype(BF16)
    row = iota((128, 256), 0)
    lane_x = iota((128, 256), 1) // 32
    third = row // 32
    x_in = (row % 32) // 4 + jnp.where(third == 1, -8, jnp.where(third == 2, 8, 0))
    pick = as_bf16((iota((128, 4), 0) % 4 == iota((128, 4), 1)) & (iota((128, 4), 0) < 96))
    for ky in range(3):
        total = jnp.zeros((128, 256), F32)
        for kx in range(3):
            tap = mm(mm(pick, w_in[3 * ky + kx]).astype(BF16), spread)
            total = jnp.where(lane_x == x_in - kx + 1, tap, total)
        w1[128 * ky : 128 * ky + 128, :] = total.astype(BF16)
    spread_t = as_bf16(iota((256, 32), 1) == iota((256, 32), 0) % 32)
    same_x = iota((256, 128), 0) // 32 == iota((256, 128), 1) % 8
    row = iota((128, 128), 0)
    for c in range(3):
        along = mm_nt(spread_t, jnp.broadcast_to(w_out[c : c + 1, :], (128, 32)))
        wo[0:256, 128 * c : 128 * c + 128] = jnp.where(same_x, along, 0.0).astype(BF16)
        own = (row < 32) & (row % 4 == c) & (row // 4 == iota((128, 128), 1) % 8)
        wo[256:384, 128 * c : 128 * c + 128] = as_bf16(own)


def ray_march(density, steps, part):
    lane = iota((64, 128), 1)
    front = lane < 64
    half = jnp.where(front, 0, 1)
    for chunk in range(density.shape[0] // 64):
        rows = slice(64 * chunk, 64 * chunk + 64)
        group = steps[:, 128 * (64 * chunk // 128) : 128 * (64 * chunk // 128) + 128].astype(F32)
        off = (64 * chunk) % 128
        eye = iota((64, 128), 0) + off == iota((64, 128), 1)
        alive = mm(jnp.where(eye, group, 0.0).astype(BF16), jnp.ones((128, 128), BF16))
        alive = alive.astype(jnp.int32)
        light = jnp.zeros((64, 128), F32)
        trans = jnp.ones((64, 128), F32)
        for j in range(4):
            sigma = density[rows, 128 * j : 128 * j + 128].astype(F32)
            keep = jnp.where(half + 2 * j < alive, jnp.exp(-STEP * sigma), 1.0)
            emit = (1.0 - keep) * sigma
            other = pltpu.roll(keep, 64, 1)
            light = light + trans * jnp.where(front, 1.0, other) * emit
            trans = trans * (keep * other)
        light = light + pltpu.roll(light, 64, 1)
        value = jnp.where(
            front, light * (LEVELS / LIGHT_TOP), (1.0 - trans) * (LEVELS / ALPHA_TOP)
        )
        part[rows, :] = split((value + 0.5).astype(jnp.int32))


def kernel(
    n_slab,
    n_tile,
    *refs,
):
    inputs, staged = refs[:11], refs[12:23]
    out, load, refs = refs[11], refs[23], refs[24:]
    loads = [
        pltpu.make_async_copy(src, dst, load.at[n])
        for n, (src, dst) in enumerate(zip(inputs, staged))
    ]
    for n in (3, 2, 1, 0, 4, 5, 6, 7, 8, 9, 10):
        loads[n].start()
    run(n_slab, n_tile, loads, *staged, out, *refs)


def run(
    n_slab,
    n_tile,
    loads,
    density,
    color,
    brick_row,
    brick_col,
    steps,
    flip,
    w_in,
    w_enc,
    w_dec,
    w_dec2,
    w_out,
    out,
    part,
    place,
    canvas_of,
    a_out,
    a_in,
    am_out,
    am_land,
    am_in,
    canvas,
    b_out,
    b_in,
    bm_out,
    bm_in,
    tint,
    h_own,
    h_edge,
    h_rows,
    h_sides,
    ext,
    x0,
    x1,
    e1,
    e2,
    d1,
    edge,
    w1,
    wb,
    wo,
    fo,
    am_send,
    am_recv,
    a_send,
    a_recv,
    bm_send,
    bm_recv,
    b_send,
    b_recv,
    h_send,
    h_recv,
):
    s = lax.axis_index("slab")
    t = lax.axis_index("tile")
    bricks = density.shape[0]
    slots = CAP * n_tile
    owned = 64 * n_slab

    def tile_peer(i):
        return (s, lax.rem(t + i, n_tile))

    def slab_peer(j):
        return (lax.rem(s + j, n_slab), t)

    def near(ds, dt):
        return (lax.rem(s + ds + n_slab, n_slab), lax.rem(t + dt + n_tile, n_tile))

    corners = [near(-1, -1), near(-1, 1), near(1, -1), near(1, 1)]
    greeted = (
        [tile_peer(i) for i in range(1, n_tile)]
        + [slab_peer(j) for j in range(1, n_slab)]
        + corners
    )
    barrier = pltpu.get_barrier_semaphore()
    for peer in greeted:
        pl.semaphore_signal(barrier, inc=1, device_id=peer, device_id_type=MESH)

    for n in (1, 2, 3):
        loads[n].wait()
    col = brick_col[...]
    row = brick_row[...]
    rel = (col // 32 - t + n_tile) % n_tile
    mine = iota((n_tile, bricks), 0) == rel
    before = as_bf16(iota((bricks, bricks), 0) < iota((bricks, bricks), 1))
    ahead = mm(as_bf16(mine), before)
    rank = jnp.sum(jnp.where(mine, ahead, 0.0), axis=0, keepdims=True).astype(jnp.int32)
    slot = rel * CAP + rank
    place[...] = as_bf16(iota((slots, bricks), 0) == slot)
    block = (row // 2 - s + n_slab) % n_slab
    tile_id = (block * 64 + row % 2 * 32 + col % 32 + 1).astype(F32)
    in_slot = iota((CAP, bricks), 0) == rank
    tints = color[...]
    fields = [tints[0:1, :], tints[1:2, :], tints[2:3, :], tile_id]
    spread = jnp.concatenate([jnp.where(in_slot, f, 0.0) for f in fields], axis=0)
    high = spread.astype(BF16)
    low = (spread - high.astype(F32)).astype(BF16)
    owner = as_bf16(mine)
    notes = mm_nt(owner, high) + mm_nt(owner, low)
    for i in range(1, n_tile):
        am_out[i] = notes[i : i + 1, :]
    am_in[0:1, :] = notes[0:1, :]

    pl.semaphore_wait(barrier, len(greeted))

    def start(src, dst, send, recv, peer):
        copy = pltpu.make_async_remote_copy(
            src_ref=src,
            dst_ref=dst,
            send_sem=send,
            recv_sem=recv,
            device_id=peer,
            device_id_type=MESH,
        )
        copy.start()
        return copy

    am_copies = [
        start(am_out.at[i], am_land.at[i], am_send.at[i], am_recv.at[i], tile_peer(i))
        for i in range(1, n_tile)
    ]

    loads[0].wait()
    loads[4].wait()
    ray_march(density, steps, part)
    a_copies = []
    for g in range(slots // 128):
        a_out[128 * g : 128 * g + 128, :] = join(
            mm(place[128 * g : 128 * g + 128, :], part[...])
        )
        for i in range(4 * g, 4 * g + 4):
            span = pl.ds(CAP * i, CAP)
            if i == 0:
                a_in[0:CAP, :] = a_out[0:CAP, :]
            else:
                a_copies.append(
                    start(
                        a_out.at[span], a_in.at[span], a_send.at[i], a_recv.at[i], tile_peer(i)
                    )
                )

    for copy in am_copies:
        copy.wait_recv()
    for i in range(1, n_tile):
        am_in[i : i + 1, :] = am_land[i]
    notes = am_in[...]
    high = notes.astype(BF16)
    both = jnp.concatenate([high, (notes - high.astype(F32)).astype(BF16)], axis=0)
    from_peer = iota((2 * n_tile, slots), 0) % n_tile == iota((2 * n_tile, slots), 1) // CAP
    in_row = iota((128, slots), 0) - iota((128, slots), 1) % CAP
    field = iota((16, slots), 0)
    arrived = jnp.zeros((16, slots), F32)
    for f in range(4):
        here = jnp.where(from_peer, mm(both, as_bf16(in_row == CAP * f)), 0.0)
        high = jnp.sum(here[0:n_tile], axis=0, keepdims=True)
        low = jnp.sum(here[n_tile:], axis=0, keepdims=True)
        if f < 3:
            arrived = jnp.where(field == 2 * f, high, jnp.where(field == 2 * f + 1, low, arrived))
        else:
            tile_id = (high + low).astype(jnp.int32) - 1
            arrived = jnp.where((field == 8) & (tile_id >= 0), 1.0, arrived)
    canvas_of[...] = as_bf16(iota((owned, slots), 0) == tile_id)
    tile_meta = mm_nt(arrived.astype(BF16), canvas_of[...]).astype(BF16)
    for g in range(n_slab // 2):
        bm_out[g] = tile_meta[:, 128 * g : 128 * g + 128]
    bm_in[0] = bm_out[0]
    bm_copies = [
        start(bm_out.at[j // 2], bm_in.at[j], bm_send.at[j], bm_recv.at[j], slab_peer(j))
        for j in range(1, n_slab)
    ]

    for n in (6, 7, 8, 9, 10):
        loads[n].wait()
    build_weights(w_in, (w_enc, w_dec, w_dec2), w_out, w1, wb, wo)
    ext[...] = jnp.zeros(ext.shape, F32)
    for ref in (x0, e1, e2, d1):
        width = ref.shape[1]
        ref[0:PAD, :] = jnp.zeros((PAD, width), F32)
        ref[ref.shape[0] - PAD :, :] = jnp.zeros((PAD, width), F32)

    chunk = min(256, slots)
    for k in range(slots // chunk):
        for i in range(max(1, k * chunk // CAP), (k + 1) * chunk // CAP):
            a_copies[i - 1].wait_recv()
        span = slice(k * chunk, (k + 1) * chunk)
        term = mm(canvas_of[:, span], split(a_in[span, :].astype(jnp.int32) + 32768))
        if k == 0:
            canvas[...] = term
        else:
            canvas[...] += term
    b_copies = []
    for j in range(n_slab):
        piece = join(canvas[64 * j : 64 * j + 64, :])
        if j == 0:
            b_in[0] = piece
        else:
            b_out[j] = piece
            b_copies.append(
                start(b_out.at[j], b_in.at[j], b_send.at[j], b_recv.at[j], slab_peer(j))
            )

    for copy in bm_copies:
        copy.wait_recv()
    lane_c = iota((16, 256), 1) // 64
    field = iota((16, 256), 0)
    choose = as_bf16(((field // 2 == lane_c) & (lane_c < 3) & (field < 6)) | ((field == 8) & (lane_c == 3)))
    for j in range(n_slab):
        both = mm_tn(bm_in[j], choose)
        tint[j] = both[64 * (j % 2) : 64 * (j % 2) + 64, :]

    loads[5].wait()
    flips = flip[pl.ds(2 * s, 2), :]
    same = iota((32, 32), 0) == iota((32, 32), 1)
    flipped = (
        jnp.concatenate(
            [
                jnp.sum(jnp.where(same, flips[r : r + 1, :], 0), axis=1, keepdims=True)
                for r in range(2)
            ],
            axis=0,
        )
        == 1
    )

    for copy in b_copies:
        copy.wait_recv()
    front = iota((64, 128), 1) < 64
    scale = scales((64, 128))
    light0 = jnp.zeros((64, 128), F32)
    light1 = jnp.zeros((64, 128), F32)
    trans = jnp.ones((64, 128), F32)
    for k in range(n_slab):
        first = lax.rem(s - k + n_slab, n_slab)
        last = lax.rem(s - (n_slab - 1 - k) + n_slab, n_slab)
        level = jnp.where(
            flipped, b_in[last].astype(jnp.int32), b_in[first].astype(jnp.int32)
        )
        piece = (level + 32768).astype(F32) * scale
        hue = jnp.where(flipped, tint[last], tint[first])
        turned = pltpu.roll(piece, 64, 1)
        part0 = (jnp.where(front, piece, turned) * hue[:, 0:128]).astype(BF16).astype(F32)
        part1 = (piece * hue[:, 128:256]).astype(BF16).astype(F32)
        alpha = jnp.where(front, pltpu.roll(part1, 64, 1), part1)
        light0 = light0 + trans * part0
        light1 = light1 + trans * part1
        trans = trans * (1.0 - alpha)
    composite = jnp.concatenate([light0, light1], axis=1).astype(BF16)
    h_own[...] = composite
    own = composite.astype(F32)
    edge_row = iota((16, 256), 0)
    for side, at in ((0, 0), (1, 31)):
        h_edge[side] = jnp.where(
            edge_row == 0,
            own[at : at + 1, :],
            jnp.where(edge_row == 1, own[at + 32 : at + 33, :], 0.0),
        ).astype(BF16)
    up, down, left, right = near(-1, 0), near(1, 0), near(0, -1), near(0, 1)
    plan = [
        (h_own.at[pl.ds(0, 32)], h_rows.at[1], up),
        (h_own.at[pl.ds(32, 32)], h_rows.at[0], down),
        (h_edge.at[0], h_sides.at[1], left),
        (h_edge.at[1], h_sides.at[0], right),
        (h_edge.at[0], h_sides.at[5], corners[0]),
        (h_edge.at[1], h_sides.at[4], corners[1]),
        (h_edge.at[0], h_sides.at[3], corners[2]),
        (h_edge.at[1], h_sides.at[2], corners[3]),
    ]
    h_copies = [
        start(src, dst, h_send.at[n], h_recv.at[n], peer) for n, (src, dst, peer) in enumerate(plan)
    ]
    has_up = jnp.where(s > 0, 1.0, 0.0)
    has_down = jnp.where(s < n_slab - 1, 1.0, 0.0)
    has_left = jnp.where(t > 0, 1.0, 0.0)
    has_right = jnp.where(t < n_tile - 1, 1.0, 0.0)
    ext[PITCH + 1 : PITCH + 33, :] = own[0:32, :]
    ext[2 * PITCH + 1 : 2 * PITCH + 33, :] = own[32:64, :]
    for copy in h_copies:
        copy.wait_recv()
    ext[1:33, :] = h_rows[0].astype(F32) * has_up
    ext[3 * PITCH + 1 : 3 * PITCH + 33, :] = h_rows[1].astype(F32) * has_down
    sides = [
        (0, has_left, ((PITCH, 0), (2 * PITCH, 1))),
        (1, has_right, ((PITCH + 33, 0), (2 * PITCH + 33, 1))),
        (2, has_up * has_left, ((0, 1),)),
        (3, has_up * has_right, ((33, 1),)),
        (4, has_down * has_left, ((3 * PITCH, 0),)),
        (5, has_down * has_right, ((3 * PITCH + 33, 0),)),
    ]
    for n, there, moves in sides:
        block = h_sides[n].astype(F32) * there
        for at, r in moves:
            ext[at : at + 1, :] = block[r : r + 1, :]

    tiles = ext[...].astype(BF16)
    lane = iota((256, 128), 1)
    source = (lane % 4) * 64 + (lane % 32) // 4
    for y in range(8):
        turn = as_bf16((iota((256, 128), 0) == source + 8 * y) & (lane < 96))
        rows = mm(tiles, turn)
        for tr in range(4):
            r = 8 * tr + y - 4
            if 0 <= r < 24:
                x0[PAD + PITCH * r : PAD + PITCH * r + PITCH, :] = rows[
                    PITCH * tr : PITCH * tr + PITCH, :
                ]
    n = 24 * PITCH
    lane = iota((n, 128), 1)
    x1[...] = jnp.where(
        lane < 32, x0[PAD : PAD + n, :], jnp.where(lane < 64, x0[PAD - 1 : PAD - 1 + n, :], x0[PAD + 1 : PAD + 1 + n, :])
    )

    group = iota((PITCH, 256), 0)
    inside = jnp.where(
        group == 0, has_left, jnp.where(group >= 33, has_right, 1.0)
    )[None]

    def finish(ref, value, outer):
        rows = value.shape[0] // PITCH
        kept = jnp.maximum(value, 0.0).reshape(rows, PITCH, 256) * inside
        ref[PAD : PAD + rows * PITCH, :] = (
            kept.reshape(rows * PITCH, 256).astype(BF16).astype(F32)
        )

        @pl.when(s == 0)
        def _():
            ref[PAD : PAD + outer * PITCH, :] = jnp.zeros((outer * PITCH, 256), F32)

        @pl.when(s == n_slab - 1)
        def _():
            ref[PAD + (rows - outer) * PITCH : PAD + rows * PITCH, :] = jnp.zeros(
                (outer * PITCH, 256), F32
            )

    m = 22 * PITCH
    wide = jnp.concatenate(
        [x1[PITCH * dy : PITCH * dy + m, :].astype(BF16) for dy in range(3)], axis=1
    )
    finish(e1, mm(wide, w1[...]), 3)

    def convolve(ref, layer, rows_in):
        n = rows_in * PITCH
        m = (rows_in - 2) * PITCH
        lane = iota((n, 128), 1)
        edge[0:n, :] = jnp.where(
            lane < 32,
            ref[PAD + 1 : PAD + 1 + n, 0:128],
            jnp.where(lane >= 96, ref[PAD - 1 : PAD - 1 + n, 128:256], 0.0),
        )
        wide = jnp.concatenate(
            [ref[PAD + PITCH * dy : PAD + PITCH * dy + m, :].astype(BF16) for dy in range(3)]
            + [edge[PITCH * dy : PITCH * dy + m, :].astype(BF16) for dy in range(3)],
            axis=1,
        )
        return mm(wide, wb[layer])

    finish(e2, convolve(e1, 0, 22), 2)
    finish(d1, convolve(e2, 1, 20), 1)
    m = 16 * PITCH
    d2 = jnp.maximum(convolve(d1, 2, 18) + e1[PAD + 3 * PITCH : PAD + 3 * PITCH + m, :], 0.0)
    last = jnp.concatenate(
        [d2.astype(BF16), x0[PAD + 4 * PITCH : PAD + 4 * PITCH + m, :].astype(BF16)], axis=1
    )
    for c in range(3):
        fo[c] = mm(last, wo[:, 128 * c : 128 * c + 128])
    of_group = iota((16, 128), 1) // 8
    for c in range(3):
        for half in range(2):
            found = jnp.zeros((16, 128), F32)
            for g in range(16):
                rows = pl.ds(1 + 16 * half + g, 16, stride=PITCH)
                found = jnp.where(of_group == g, fo[c, rows, :], found)
            out[c, :, 128 * half : 128 * half + 128] = found.astype(BF16)

    for copy in am_copies + a_copies + bm_copies + b_copies + h_copies:
        copy.wait_send()


def shards(
    density,
    brick_color,
    brick_row,
    brick_col,
    brick_steps,
    depth_flip,
    w_in,
    w_enc,
    w_dec,
    w_dec2,
    w_out,
):
    n_tile = lax.axis_size("tile")
    n_slab = lax.axis_size("slab")
    bricks = density.shape[0]
    slots = CAP * n_tile
    owned = 64 * n_slab
    taps = [jnp.transpose(w, (2, 3, 0, 1)).reshape(288, 32) for w in (w_enc, w_dec, w_dec2)]
    vmem = pl.BlockSpec(memory_space=pltpu.VMEM)
    dma = pltpu.SemaphoreType.DMA
    operands = (
        density,
        brick_color,
        brick_row.reshape(1, bricks),
        brick_col.reshape(1, bricks),
        brick_steps.reshape(1, bricks),
        depth_flip,
        jnp.transpose(w_in, (2, 3, 1, 0)).reshape(9, 4, 32),
        *taps,
        w_out,
    )
    return pl.pallas_call(
        functools.partial(kernel, n_slab, n_tile),
        out_shape=jax.ShapeDtypeStruct((3, 16, 256), BF16),
        in_specs=[pl.BlockSpec(memory_space=pltpu.HBM)] * 11,
        out_specs=vmem,
        scratch_shapes=[pltpu.VMEM(x.shape, x.dtype) for x in operands]
        + [
            dma((11,)),
            pltpu.VMEM((bricks, 256), BF16),
            pltpu.VMEM((slots, bricks), BF16),
            pltpu.VMEM((owned, slots), BF16),
            pltpu.VMEM((slots, 128), jnp.int16),
            pltpu.VMEM((slots, 128), jnp.int16),
            pltpu.VMEM((n_tile, 1, 128), F32),
            pltpu.VMEM((n_tile, 1, 128), F32),
            pltpu.VMEM((n_tile, 128), F32),
            pltpu.VMEM((owned, 256), F32),
            pltpu.VMEM((n_slab, 64, 128), jnp.int16),
            pltpu.VMEM((n_slab, 64, 128), jnp.int16),
            pltpu.VMEM((n_slab // 2, 16, 128), BF16),
            pltpu.VMEM((n_slab, 16, 128), BF16),
            pltpu.VMEM((n_slab, 64, 256), F32),
            pltpu.VMEM((64, 256), BF16),
            pltpu.VMEM((2, 16, 256), BF16),
            pltpu.VMEM((2, 32, 256), BF16),
            pltpu.VMEM((6, 16, 256), BF16),
            pltpu.VMEM((4 * PITCH, 256), F32),
            pltpu.VMEM((24 * PITCH + 2 * PAD, 128), F32),
            pltpu.VMEM((24 * PITCH, 128), F32),
            pltpu.VMEM((22 * PITCH + 2 * PAD, 256), F32),
            pltpu.VMEM((20 * PITCH + 2 * PAD, 256), F32),
            pltpu.VMEM((18 * PITCH + 2 * PAD, 256), F32),
            pltpu.VMEM((22 * PITCH, 128), F32),
            pltpu.VMEM((384, 256), BF16),
            pltpu.VMEM((3, 1152, 256), BF16),
            pltpu.VMEM((384, 384), BF16),
            pltpu.VMEM((3, 16 * PITCH, 128), F32),
            dma((n_tile,)),
            dma((n_tile,)),
            dma((n_tile,)),
            dma((n_tile,)),
            dma((n_slab,)),
            dma((n_slab,)),
            dma((n_slab,)),
            dma((n_slab,)),
            dma((8,)),
            dma((8,)),
        ],
        compiler_params=pltpu.CompilerParams(
            collective_id=0, has_side_effects=True, vmem_limit_bytes=62 * 1024 * 1024
        ),
    )(*operands)


def solution(mesh):
    return jax.shard_map(
        shards,
        mesh=mesh,
        in_specs=(
            P(("slab", "tile"), None),
            P(None, ("slab", "tile")),
            P(("slab", "tile")),
            P(("slab", "tile")),
            P(("slab", "tile")),
            P(None, "tile"),
            P(),
            P(),
            P(),
            P(),
            P(),
        ),
        out_specs=P(None, "slab", "tile"),
        check_vma=False,
    )
```

```python
import functools
import jax
import jax.numpy as jnp
from jax import lax
from jax.experimental import pallas as pl
from jax.experimental.pallas import tpu as pltpu
from jax.sharding import PartitionSpec as P

MESH = pl.DeviceIdType.MESH
BF16 = jnp.bfloat16
F32 = jnp.float32
STEP = 0.03
CAP = 32
PITCH = 40
PAD = 8
LIGHT_TOP = 2.5
ALPHA_TOP = 0.625
LEVELS = 65535.0


def iota(shape, dim):
    return lax.broadcasted_iota(jnp.int32, shape, dim)


def as_bf16(cond):
    return jnp.where(cond, 1.0, 0.0).astype(BF16)


def mm(a, b):
    return jnp.dot(a, b, preferred_element_type=F32)


def mm_nt(a, b):
    return lax.dot_general(a, b, (((1,), (1,)), ((), ())), preferred_element_type=F32)


def mm_tn(a, b):
    return lax.dot_general(a, b, (((0,), (0,)), ((), ())), preferred_element_type=F32)


def scales(shape):
    front = iota(shape, 1) < 64
    return jnp.where(front, LIGHT_TOP / LEVELS, ALPHA_TOP / LEVELS)


def split(levels):
    high = levels // 256
    low = levels - 256 * high
    return jnp.concatenate([high.astype(F32), low.astype(F32)], axis=1).astype(BF16)


def join(halves):
    levels = (256.0 * halves[:, 0:128] + halves[:, 128:256]).astype(jnp.int32)
    return (levels - 32768).astype(jnp.int16)


def build_weights(w_in, w_layers, w_out, w1, wb, wo):
    spread = as_bf16(iota((32, 256), 0) == iota((32, 256), 1) % 32)
    lane_x = iota((32, 256), 1) // 32
    for layer, w_ref in enumerate(w_layers):
        turned = jnp.transpose(w_ref[...].astype(F32))
        for ky in range(3):
            taps = [
                mm(turned[:, 32 * (3 * ky + kx) : 32 * (3 * ky + kx) + 32].astype(BF16), spread)
                for kx in range(3)
            ]
            base = 256 * ky
            for x_in in range(8):
                total = jnp.zeros((32, 256), F32)
                for kx in range(3):
                    total = jnp.where(lane_x == x_in - kx + 1, taps[kx], total)
                wb[layer, base + 32 * x_in : base + 32 * x_in + 32, :] = total.astype(BF16)
            edge = 768 + 128 * ky
            wb[layer, edge : edge + 32, :] = jnp.where(lane_x == 7, taps[2], 0.0).astype(BF16)
            wb[layer, edge + 32 : edge + 96, :] = jnp.zeros((64, 256), BF16)
            wb[layer, edge + 96 : edge + 128, :] = jnp.where(lane_x == 0, taps[0], 0.0).astype(BF16)
    row = iota((128, 256), 0)
    lane_x = iota((128, 256), 1) // 32
    third = row // 32
    x_in = (row % 32) // 4 + jnp.where(third == 1, -8, jnp.where(third == 2, 8, 0))
    pick = as_bf16((iota((128, 4), 0) % 4 == iota((128, 4), 1)) & (iota((128, 4), 0) < 96))
    for ky in range(3):
        total = jnp.zeros((128, 256), F32)
        for kx in range(3):
            tap = mm(mm(pick, w_in[3 * ky + kx]).astype(BF16), spread)
            total = jnp.where(lane_x == x_in - kx + 1, tap, total)
        w1[128 * ky : 128 * ky + 128, :] = total.astype(BF16)
    spread_t = as_bf16(iota((256, 32), 1) == iota((256, 32), 0) % 32)
    same_x = iota((256, 128), 0) // 32 == iota((256, 128), 1) % 8
    row = iota((128, 128), 0)
    for c in range(3):
        along = mm_nt(spread_t, jnp.broadcast_to(w_out[c : c + 1, :], (128, 32)))
        wo[0:256, 128 * c : 128 * c + 128] = jnp.where(same_x, along, 0.0).astype(BF16)
        own = (row < 32) & (row % 4 == c) & (row // 4 == iota((128, 128), 1) % 8)
        wo[256:384, 128 * c : 128 * c + 128] = as_bf16(own)


def ray_march(density, steps, part):
    lane = iota((64, 128), 1)
    front = lane < 64
    half = jnp.where(front, 0, 1)
    for chunk in range(density.shape[0] // 64):
        rows = slice(64 * chunk, 64 * chunk + 64)
        group = steps[:, 128 * (64 * chunk // 128) : 128 * (64 * chunk // 128) + 128].astype(F32)
        off = (64 * chunk) % 128
        eye = iota((64, 128), 0) + off == iota((64, 128), 1)
        alive = mm(jnp.where(eye, group, 0.0).astype(BF16), jnp.ones((128, 128), BF16))
        alive = alive.astype(jnp.int32)
        light = jnp.zeros((64, 128), F32)
        trans = jnp.ones((64, 128), F32)
        for j in range(4):
            sigma = density[rows, 128 * j : 128 * j + 128].astype(F32)
            keep = jnp.where(half + 2 * j < alive, jnp.exp(-STEP * sigma), 1.0)
            emit = (1.0 - keep) * sigma
            other = pltpu.roll(keep, 64, 1)
            light = light + trans * jnp.where(front, 1.0, other) * emit
            trans = trans * (keep * other)
        light = light + pltpu.roll(light, 64, 1)
        value = jnp.where(
            front, light * (LEVELS / LIGHT_TOP), (1.0 - trans) * (LEVELS / ALPHA_TOP)
        )
        part[rows, :] = split((value + 0.5).astype(jnp.int32))


def denoise(
    top, bottom, has_left, has_right, ext, x0, x1, e1, e2, d1, edge, w1, wb, wo, fo, out
):
    tiles = ext[...].astype(BF16)
    lane = iota((256, 128), 1)
    source = (lane % 4) * 64 + (lane % 32) // 4
    for y in range(8):
        turn = as_bf16((iota((256, 128), 0) == source + 8 * y) & (lane < 96))
        rows = mm(tiles, turn)
        for tr in range(4):
            r = 8 * tr + y - 4
            if 0 <= r < 24:
                x0[PAD + PITCH * r : PAD + PITCH * r + PITCH, :] = rows[
                    PITCH * tr : PITCH * tr + PITCH, :
                ]
    n = 24 * PITCH
    lane = iota((n, 128), 1)
    x1[...] = jnp.where(
        lane < 32, x0[PAD : PAD + n, :], jnp.where(lane < 64, x0[PAD - 1 : PAD - 1 + n, :], x0[PAD + 1 : PAD + 1 + n, :])
    )

    group = iota((PITCH, 256), 0)
    inside = jnp.where(
        group == 0, has_left, jnp.where(group >= 33, has_right, 1.0)
    )[None]

    def finish(ref, value, outer):
        rows = value.shape[0] // PITCH
        kept = jnp.maximum(value, 0.0).reshape(rows, PITCH, 256) * inside
        ref[PAD : PAD + rows * PITCH, :] = (
            kept.reshape(rows * PITCH, 256).astype(BF16).astype(F32)
        )

        @pl.when(top)
        def _():
            ref[PAD : PAD + outer * PITCH, :] = jnp.zeros((outer * PITCH, 256), F32)

        @pl.when(bottom)
        def _():
            ref[PAD + (rows - outer) * PITCH : PAD + rows * PITCH, :] = jnp.zeros(
                (outer * PITCH, 256), F32
            )

    m = 22 * PITCH
    wide = jnp.concatenate(
        [x1[PITCH * dy : PITCH * dy + m, :].astype(BF16) for dy in range(3)], axis=1
    )
    finish(e1, mm(wide, w1[...]), 3)

    def convolve(ref, layer, rows_in):
        n = rows_in * PITCH
        m = (rows_in - 2) * PITCH
        lane = iota((n, 128), 1)
        edge[0:n, :] = jnp.where(
            lane < 32,
            ref[PAD + 1 : PAD + 1 + n, 0:128],
            jnp.where(lane >= 96, ref[PAD - 1 : PAD - 1 + n, 128:256], 0.0),
        )
        wide = jnp.concatenate(
            [ref[PAD + PITCH * dy : PAD + PITCH * dy + m, :].astype(BF16) for dy in range(3)]
            + [edge[PITCH * dy : PITCH * dy + m, :].astype(BF16) for dy in range(3)],
            axis=1,
        )
        return mm(wide, wb[layer])

    finish(e2, convolve(e1, 0, 22), 2)
    finish(d1, convolve(e2, 1, 20), 1)
    m = 16 * PITCH
    d2 = jnp.maximum(convolve(d1, 2, 18) + e1[PAD + 3 * PITCH : PAD + 3 * PITCH + m, :], 0.0)
    last = jnp.concatenate(
        [d2.astype(BF16), x0[PAD + 4 * PITCH : PAD + 4 * PITCH + m, :].astype(BF16)], axis=1
    )
    for c in range(3):
        fo[c] = mm(last, wo[:, 128 * c : 128 * c + 128])
    of_group = iota((16, 128), 1) // 8
    for c in range(3):
        for half in range(2):
            found = jnp.zeros((16, 128), F32)
            for g in range(16):
                rows = pl.ds(1 + 16 * half + g, 16, stride=PITCH)
                found = jnp.where(of_group == g, fo[c, rows, :], found)
            out[c, :, 128 * half : 128 * half + 128] = found.astype(BF16)


def kernel(
    n_slab,
    n_tile,
    *refs,
):
    inputs, staged = refs[:11], refs[12:23]
    out, load, refs = refs[11], refs[23], refs[24:]
    loads = [
        pltpu.make_async_copy(src, dst, load.at[n])
        for n, (src, dst) in enumerate(zip(inputs, staged))
    ]
    run(n_slab, n_tile, loads, *staged, out, *refs)


def run(
    n_slab,
    n_tile,
    loads,
    density,
    color,
    brick_row,
    brick_col,
    steps,
    flip,
    w_in,
    w_enc,
    w_dec,
    w_dec2,
    w_out,
    out,
    part,
    place,
    canvas_of,
    a_out,
    a_in,
    am_out,
    am_land,
    am_in,
    canvas,
    b_out,
    b_in,
    bm_out,
    bm_in,
    tint,
    h_own,
    h_edge,
    h_rows,
    h_sides,
    ext,
    x0,
    x1,
    e1,
    e2,
    d1,
    edge,
    w1,
    wb,
    wo,
    fo,
    am_send,
    am_recv,
    a_send,
    a_recv,
    bm_send,
    bm_recv,
    b_send,
    b_recv,
    h_send,
    h_recv,
):
    s = lax.axis_index("slab")
    t = lax.axis_index("tile")
    bricks = density.shape[0]
    slots = CAP * n_tile
    owned = 64 * n_slab

    def tile_peer(i):
        return (s, lax.rem(t + i, n_tile))

    def slab_peer(j):
        return (lax.rem(s + j, n_slab), t)

    def near(ds, dt):
        return (lax.rem(s + ds + n_slab, n_slab), lax.rem(t + dt + n_tile, n_tile))

    corners = [near(-1, -1), near(-1, 1), near(1, -1), near(1, 1)]
    greeted = (
        [tile_peer(i) for i in range(1, n_tile)]
        + [slab_peer(j) for j in range(1, n_slab)]
        + corners
    )
    barrier = pltpu.get_barrier_semaphore()
    for peer in greeted:
        pl.semaphore_signal(barrier, inc=1, device_id=peer, device_id_type=MESH)

    for n in (3, 2, 1, 0, 4, 5, 6, 7, 8, 9, 10):
        loads[n].start()
    for n in (1, 2, 3):
        loads[n].wait()
    col = brick_col[...]
    row = brick_row[...]
    rel = (col // 32 - t + n_tile) % n_tile
    mine = iota((n_tile, bricks), 0) == rel
    before = as_bf16(iota((bricks, bricks), 0) < iota((bricks, bricks), 1))
    ahead = mm(as_bf16(mine), before)
    rank = jnp.sum(jnp.where(mine, ahead, 0.0), axis=0, keepdims=True).astype(jnp.int32)
    slot = rel * CAP + rank
    place[...] = as_bf16(iota((slots, bricks), 0) == slot)
    block = (row // 2 - s + n_slab) % n_slab
    tile_id = (block * 64 + row % 2 * 32 + col % 32 + 1).astype(F32)
    in_slot = iota((CAP, bricks), 0) == rank
    tints = color[...]
    fields = [tints[0:1, :], tints[1:2, :], tints[2:3, :], tile_id]
    spread = jnp.concatenate([jnp.where(in_slot, f, 0.0) for f in fields], axis=0)
    high = spread.astype(BF16)
    low = (spread - high.astype(F32)).astype(BF16)
    owner = as_bf16(mine)
    notes = mm_nt(owner, high) + mm_nt(owner, low)
    for i in range(1, n_tile):
        am_out[i] = notes[i : i + 1, :]
    am_in[0:1, :] = notes[0:1, :]

    def start(src, dst, send, recv, peer):
        copy = pltpu.make_async_remote_copy(
            src_ref=src,
            dst_ref=dst,
            send_sem=send,
            recv_sem=recv,
            device_id=peer,
            device_id_type=MESH,
        )
        copy.start()
        return copy

    loads[0].wait()
    loads[4].wait()
    ray_march(density, steps, part)
    for g in range(slots // 128):
        a_out[128 * g : 128 * g + 128, :] = join(
            mm(place[128 * g : 128 * g + 128, :], part[...])
        )
    a_in[0:CAP, :] = a_out[0:CAP, :]

    pl.semaphore_wait(barrier, len(greeted))
    across = range(1, n_tile)
    am_copies = {
        i: start(am_out.at[i], am_land.at[i], am_send.at[i], am_recv.at[i], tile_peer(i))
        for i in across
    }
    a_copies = {}
    for i in across:
        span = pl.ds(CAP * i, CAP)
        a_copies[i] = start(
            a_out.at[span], a_in.at[span], a_send.at[i], a_recv.at[i], tile_peer(i)
        )

    for n in (6, 7, 8, 9, 10):
        loads[n].wait()
    build_weights(w_in, (w_enc, w_dec, w_dec2), w_out, w1, wb, wo)
    ext[...] = jnp.zeros(ext.shape, F32)
    for ref in (x0, e1, e2, d1):
        width = ref.shape[1]
        ref[0:PAD, :] = jnp.zeros((PAD, width), F32)
        ref[ref.shape[0] - PAD :, :] = jnp.zeros((PAD, width), F32)

    for i in range(1, n_tile):
        am_copies[i].wait_recv()
        am_in[i : i + 1, :] = am_land[i]
    notes = am_in[...]
    high = notes.astype(BF16)
    both = jnp.concatenate([high, (notes - high.astype(F32)).astype(BF16)], axis=0)
    from_peer = iota((2 * n_tile, slots), 0) % n_tile == iota((2 * n_tile, slots), 1) // CAP
    in_row = iota((128, slots), 0) - iota((128, slots), 1) % CAP
    field = iota((16, slots), 0)
    arrived = jnp.zeros((16, slots), F32)
    for f in range(4):
        here = jnp.where(from_peer, mm(both, as_bf16(in_row == CAP * f)), 0.0)
        high = jnp.sum(here[0:n_tile], axis=0, keepdims=True)
        low = jnp.sum(here[n_tile:], axis=0, keepdims=True)
        if f < 3:
            arrived = jnp.where(field == 2 * f, high, jnp.where(field == 2 * f + 1, low, arrived))
        else:
            tile_id = (high + low).astype(jnp.int32) - 1
            arrived = jnp.where((field == 8) & (tile_id >= 0), 1.0, arrived)
    canvas_of[...] = as_bf16(iota((owned, slots), 0) == tile_id)
    tile_meta = mm_nt(arrived.astype(BF16), canvas_of[...]).astype(BF16)
    for g in range(n_slab // 2):
        bm_out[g] = tile_meta[:, 128 * g : 128 * g + 128]
    bm_in[0] = bm_out[0]
    bm_copies = [
        start(bm_out.at[j // 2], bm_in.at[j], bm_send.at[j], bm_recv.at[j], slab_peer(j))
        for j in range(1, n_slab)
    ]

    chunk = min(256, slots)
    spans = [slice(k * chunk, (k + 1) * chunk) for k in (0, 1, 3, 2) if k * chunk < slots]
    for k, span in enumerate(spans):
        for i in range(max(1, span.start // CAP), span.stop // CAP):
            a_copies[i].wait_recv()
        came = split(a_in[span, :].astype(jnp.int32) + 32768)
        if k + 1 < len(spans):
            term = mm(canvas_of[:, span], came)
            if k == 0:
                canvas[...] = term
            else:
                canvas[...] += term
    b_copies = []
    for pair in range(n_slab // 2):
        rows = slice(128 * pair, 128 * pair + 128)
        levels = mm(canvas_of[rows, span], came)
        if len(spans) > 1:
            levels = levels + canvas[rows, :]
        levels = join(levels)
        for j in (2 * pair, 2 * pair + 1):
            piece = levels[64 * (j % 2) : 64 * (j % 2) + 64, :]
            if j == 0:
                b_in[0] = piece
            else:
                b_out[j] = piece
                b_copies.append(
                    start(b_out.at[j], b_in.at[j], b_send.at[j], b_recv.at[j], slab_peer(j))
                )

    for copy in bm_copies:
        copy.wait_recv()
    lane_c = iota((16, 256), 1) // 64
    field = iota((16, 256), 0)
    choose = as_bf16(((field // 2 == lane_c) & (lane_c < 3) & (field < 6)) | ((field == 8) & (lane_c == 3)))
    for j in range(n_slab):
        both = mm_tn(bm_in[j], choose)
        tint[j] = both[64 * (j % 2) : 64 * (j % 2) + 64, :]

    loads[5].wait()
    flips = flip[pl.ds(2 * s, 2), :]
    same = iota((32, 32), 0) == iota((32, 32), 1)
    flipped = (
        jnp.concatenate(
            [
                jnp.sum(jnp.where(same, flips[r : r + 1, :], 0), axis=1, keepdims=True)
                for r in range(2)
            ],
            axis=0,
        )
        == 1
    )

    for copy in b_copies:
        copy.wait_recv()
    front = iota((64, 128), 1) < 64
    scale = scales((64, 128))
    light0 = jnp.zeros((64, 128), F32)
    light1 = jnp.zeros((64, 128), F32)
    trans = jnp.ones((64, 128), F32)
    for k in range(n_slab):
        first = lax.rem(s - k + n_slab, n_slab)
        last = lax.rem(s - (n_slab - 1 - k) + n_slab, n_slab)
        level = jnp.where(
            flipped, b_in[last].astype(jnp.int32), b_in[first].astype(jnp.int32)
        )
        piece = (level + 32768).astype(F32) * scale
        hue = jnp.where(flipped, tint[last], tint[first])
        turned = pltpu.roll(piece, 64, 1)
        part0 = (jnp.where(front, piece, turned) * hue[:, 0:128]).astype(BF16).astype(F32)
        part1 = (piece * hue[:, 128:256]).astype(BF16).astype(F32)
        alpha = jnp.where(front, pltpu.roll(part1, 64, 1), part1)
        light0 = light0 + trans * part0
        light1 = light1 + trans * part1
        trans = trans * (1.0 - alpha)
    composite = jnp.concatenate([light0, light1], axis=1).astype(BF16)
    h_own[...] = composite
    own = composite.astype(F32)
    edge_row = iota((16, 256), 0)
    for side, at in ((0, 0), (1, 31)):
        h_edge[side] = jnp.where(
            edge_row == 0,
            own[at : at + 1, :],
            jnp.where(edge_row == 1, own[at + 32 : at + 33, :], 0.0),
        ).astype(BF16)
    up, down, left, right = near(-1, 0), near(1, 0), near(0, -1), near(0, 1)
    plan = [
        (h_edge.at[0], h_sides.at[5], corners[0]),
        (h_edge.at[1], h_sides.at[4], corners[1]),
        (h_edge.at[0], h_sides.at[3], corners[2]),
        (h_edge.at[1], h_sides.at[2], corners[3]),
        (h_edge.at[0], h_sides.at[1], left),
        (h_edge.at[1], h_sides.at[0], right),
        (h_own.at[pl.ds(0, 32)], h_rows.at[1], up),
        (h_own.at[pl.ds(32, 32)], h_rows.at[0], down),
    ]
    h_copies = [
        start(src, dst, h_send.at[n], h_recv.at[n], peer) for n, (src, dst, peer) in enumerate(plan)
    ]
    has_up = jnp.where(s > 0, 1.0, 0.0)
    has_down = jnp.where(s < n_slab - 1, 1.0, 0.0)
    has_left = jnp.where(t > 0, 1.0, 0.0)
    has_right = jnp.where(t < n_tile - 1, 1.0, 0.0)
    ext[PITCH + 1 : PITCH + 33, :] = own[0:32, :]
    ext[2 * PITCH + 1 : 2 * PITCH + 33, :] = own[32:64, :]
    for copy in h_copies:
        copy.wait_recv()
    ext[1:33, :] = h_rows[0].astype(F32) * has_up
    ext[3 * PITCH + 1 : 3 * PITCH + 33, :] = h_rows[1].astype(F32) * has_down
    sides = [
        (0, has_left, ((PITCH, 0), (2 * PITCH, 1))),
        (1, has_right, ((PITCH + 33, 0), (2 * PITCH + 33, 1))),
        (2, has_up * has_left, ((0, 1),)),
        (3, has_up * has_right, ((33, 1),)),
        (4, has_down * has_left, ((3 * PITCH, 0),)),
        (5, has_down * has_right, ((3 * PITCH + 33, 0),)),
    ]
    for n, there, moves in sides:
        block = h_sides[n].astype(F32) * there
        for at, r in moves:
            ext[at : at + 1, :] = block[r : r + 1, :]

    denoise(
        s == 0, s == n_slab - 1, has_left, has_right, ext, x0, x1, e1, e2, d1, edge, w1, wb, wo, fo, out
    )

    for copy in [*am_copies.values(), *a_copies.values()] + bm_copies + b_copies + h_copies:
        copy.wait_send()


def shards(
    density,
    brick_color,
    brick_row,
    brick_col,
    brick_steps,
    depth_flip,
    w_in,
    w_enc,
    w_dec,
    w_dec2,
    w_out,
):
    n_tile = lax.axis_size("tile")
    n_slab = lax.axis_size("slab")
    bricks = density.shape[0]
    slots = CAP * n_tile
    owned = 64 * n_slab
    taps = [jnp.transpose(w, (2, 3, 0, 1)).reshape(288, 32) for w in (w_enc, w_dec, w_dec2)]
    vmem = pl.BlockSpec(memory_space=pltpu.VMEM)
    dma = pltpu.SemaphoreType.DMA
    operands = (
        density,
        brick_color,
        brick_row.reshape(1, bricks),
        brick_col.reshape(1, bricks),
        brick_steps.reshape(1, bricks),
        depth_flip,
        jnp.transpose(w_in, (2, 3, 1, 0)).reshape(9, 4, 32),
        *taps,
        w_out,
    )
    return pl.pallas_call(
        functools.partial(kernel, n_slab, n_tile),
        out_shape=jax.ShapeDtypeStruct((3, 16, 256), BF16),
        in_specs=[pl.BlockSpec(memory_space=pltpu.HBM)] * 11,
        out_specs=vmem,
        scratch_shapes=[pltpu.VMEM(x.shape, x.dtype) for x in operands]
        + [
            dma((11,)),
            pltpu.VMEM((bricks, 256), BF16),
            pltpu.VMEM((slots, bricks), BF16),
            pltpu.VMEM((owned, slots), BF16),
            pltpu.VMEM((slots, 128), jnp.int16),
            pltpu.VMEM((slots, 128), jnp.int16),
            pltpu.VMEM((n_tile, 1, 128), F32),
            pltpu.VMEM((n_tile, 1, 128), F32),
            pltpu.VMEM((n_tile, 128), F32),
            pltpu.VMEM((owned, 256), F32),
            pltpu.VMEM((n_slab, 64, 128), jnp.int16),
            pltpu.VMEM((n_slab, 64, 128), jnp.int16),
            pltpu.VMEM((n_slab // 2, 16, 128), BF16),
            pltpu.VMEM((n_slab, 16, 128), BF16),
            pltpu.VMEM((n_slab, 64, 256), F32),
            pltpu.VMEM((64, 256), BF16),
            pltpu.VMEM((2, 16, 256), BF16),
            pltpu.VMEM((2, 32, 256), BF16),
            pltpu.VMEM((6, 16, 256), BF16),
            pltpu.VMEM((4 * PITCH, 256), F32),
            pltpu.VMEM((24 * PITCH + 2 * PAD, 128), F32),
            pltpu.VMEM((24 * PITCH, 128), F32),
            pltpu.VMEM((22 * PITCH + 2 * PAD, 256), F32),
            pltpu.VMEM((20 * PITCH + 2 * PAD, 256), F32),
            pltpu.VMEM((18 * PITCH + 2 * PAD, 256), F32),
            pltpu.VMEM((22 * PITCH, 128), F32),
            pltpu.VMEM((384, 256), BF16),
            pltpu.VMEM((3, 1152, 256), BF16),
            pltpu.VMEM((384, 384), BF16),
            pltpu.VMEM((3, 16 * PITCH, 128), F32),
            dma((n_tile,)),
            dma((n_tile,)),
            dma((n_tile,)),
            dma((n_tile,)),
            dma((n_slab,)),
            dma((n_slab,)),
            dma((n_slab,)),
            dma((n_slab,)),
            dma((8,)),
            dma((8,)),
        ],
        compiler_params=pltpu.CompilerParams(
            collective_id=0, has_side_effects=True, vmem_limit_bytes=62 * 1024 * 1024
        ),
    )(*operands)


def solution(mesh):
    return jax.shard_map(
        shards,
        mesh=mesh,
        in_specs=(
            P(("slab", "tile"), None),
            P(None, ("slab", "tile")),
            P(("slab", "tile")),
            P(("slab", "tile")),
            P(("slab", "tile")),
            P(None, "tile"),
            P(),
            P(),
            P(),
            P(),
            P(),
        ),
        out_specs=P(None, "slab", "tile"),
        check_vma=False,
    )
```

```python
import functools
import jax
import jax.numpy as jnp
from jax import lax
from jax.experimental import pallas as pl
from jax.experimental.pallas import tpu as pltpu
from jax.sharding import PartitionSpec as P

MESH = pl.DeviceIdType.MESH
BF16 = jnp.bfloat16
F32 = jnp.float32
STEP = 0.03
CAP = 32
PITCH = 40
PAD = 8
LIGHT_TOP = 2.5
ALPHA_TOP = 0.625
LEVELS = 65535.0


def iota(shape, dim):
    return lax.broadcasted_iota(jnp.int32, shape, dim)


def as_bf16(cond):
    return jnp.where(cond, 1.0, 0.0).astype(BF16)


def mm(a, b):
    return jnp.dot(a, b, preferred_element_type=F32)


def mm_nt(a, b):
    return lax.dot_general(a, b, (((1,), (1,)), ((), ())), preferred_element_type=F32)


def mm_tn(a, b):
    return lax.dot_general(a, b, (((0,), (0,)), ((), ())), preferred_element_type=F32)


def scales(shape):
    front = iota(shape, 1) < 64
    return jnp.where(front, LIGHT_TOP / LEVELS, ALPHA_TOP / LEVELS)


def split(levels):
    high = levels // 256
    low = levels - 256 * high
    return jnp.concatenate([high.astype(F32), low.astype(F32)], axis=1).astype(BF16)


def join(halves):
    levels = (256.0 * halves[:, 0:128] + halves[:, 128:256]).astype(jnp.int32)
    return (levels - 32768).astype(jnp.int16)


def build_weights(w_in, w_layers, w_out, w1, wb, wo):
    spread = as_bf16(iota((32, 256), 0) == iota((32, 256), 1) % 32)
    lane_x = iota((32, 256), 1) // 32
    for layer, w_ref in enumerate(w_layers):
        turned = jnp.transpose(w_ref[...].astype(F32))
        for ky in range(3):
            taps = [
                mm(turned[:, 32 * (3 * ky + kx) : 32 * (3 * ky + kx) + 32].astype(BF16), spread)
                for kx in range(3)
            ]
            base = 256 * ky
            for x_in in range(8):
                total = jnp.zeros((32, 256), F32)
                for kx in range(3):
                    total = jnp.where(lane_x == x_in - kx + 1, taps[kx], total)
                wb[layer, base + 32 * x_in : base + 32 * x_in + 32, :] = total.astype(BF16)
            right, left = ((768, 864), (832, 800), (896, 992))[ky]
            wb[layer, right : right + 32, :] = jnp.where(lane_x == 7, taps[2], 0.0).astype(BF16)
            wb[layer, left : left + 32, :] = jnp.where(lane_x == 0, taps[0], 0.0).astype(BF16)
        wb[layer, 928:992, :] = jnp.zeros((64, 256), BF16)
    row = iota((128, 256), 0)
    lane_x = iota((128, 256), 1) // 32
    third = row // 32
    x_in = (row % 32) // 4 + jnp.where(third == 1, -8, jnp.where(third == 2, 8, 0))
    pick = as_bf16((iota((128, 4), 0) % 4 == iota((128, 4), 1)) & (iota((128, 4), 0) < 96))
    for ky in range(3):
        total = jnp.zeros((128, 256), F32)
        for kx in range(3):
            tap = mm(mm(pick, w_in[3 * ky + kx]).astype(BF16), spread)
            total = jnp.where(lane_x == x_in - kx + 1, tap, total)
        w1[128 * ky : 128 * ky + 128, :] = total.astype(BF16)
    spread_t = as_bf16(iota((256, 32), 1) == iota((256, 32), 0) % 32)
    same_x = iota((256, 128), 0) // 32 == iota((256, 128), 1) % 8
    for c in range(3):
        along = mm_nt(spread_t, jnp.broadcast_to(w_out[c : c + 1, :], (128, 32)))
        wo[0:256, 128 * c : 128 * c + 128] = jnp.where(same_x, along, 0.0).astype(BF16)


def ray_march(density, steps, part):
    lane = iota((64, 128), 1)
    front = lane < 64
    half = jnp.where(front, 0, 1)
    for chunk in range(density.shape[0] // 64):
        rows = slice(64 * chunk, 64 * chunk + 64)
        group = steps[:, 128 * (64 * chunk // 128) : 128 * (64 * chunk // 128) + 128].astype(F32)
        off = (64 * chunk) % 128
        eye = iota((64, 128), 0) + off == iota((64, 128), 1)
        alive = mm(jnp.where(eye, group, 0.0).astype(BF16), jnp.ones((128, 128), BF16))
        alive = alive.astype(jnp.int32)
        light = jnp.zeros((64, 128), F32)
        trans = jnp.ones((64, 128), F32)
        for j in range(4):
            sigma = density[rows, 128 * j : 128 * j + 128].astype(F32)
            keep = jnp.where(half + 2 * j < alive, jnp.exp(-STEP * sigma), 1.0)
            emit = (1.0 - keep) * sigma
            other = pltpu.roll(keep, 64, 1)
            light = light + trans * jnp.where(front, 1.0, other) * emit
            trans = trans * (keep * other)
        light = light + pltpu.roll(light, 64, 1)
        value = jnp.where(
            front, light * (LEVELS / LIGHT_TOP), (1.0 - trans) * (LEVELS / ALPHA_TOP)
        )
        part[rows, :] = split((value + 0.5).astype(jnp.int32))


def lay_out(tiles, base):
    row = iota((256, 384), 0)
    lane = iota((256, 384), 1)
    source = lane // 128 * 64 + lane % 8
    of_tile = iota((16, 128), 0) == iota((16, 128), 1) // 8
    for y in range(8):
        spread = mm(tiles, as_bf16(row == source + 8 * y))
        for tr in range(2):
            for half in range(2):
                first = 32 * tr + 16 * half
                for c in range(3):
                    block = spread[first : first + 16, 128 * c : 128 * c + 128]
                    base[c, 8 * tr + y : 8 * tr + y + 1, 128 * half : 128 * half + 128] = jnp.sum(
                        jnp.where(of_tile, block, 0.0), axis=0, keepdims=True
                    )


def denoise(
    top, bottom, has_left, has_right, ext, x0, x1, e1, e2, d1, edge, w1, wb, wo, fo, base, out
):
    tiles = ext[...].astype(BF16)
    lane = iota((256, 128), 1)
    source = (lane % 4) * 64 + (lane % 32) // 4
    for y in range(8):
        turn = as_bf16((iota((256, 128), 0) == source + 8 * y) & (lane < 96))
        rows = mm(tiles, turn)
        for tr in range(4):
            r = 8 * tr + y - 4
            if 0 <= r < 24:
                x0[PAD + PITCH * r : PAD + PITCH * r + PITCH, :] = rows[
                    PITCH * tr : PITCH * tr + PITCH, :
                ]
    n = 24 * PITCH
    lane = iota((n, 128), 1)
    x1[...] = jnp.where(
        lane < 32, x0[PAD : PAD + n, :], jnp.where(lane < 64, x0[PAD - 1 : PAD - 1 + n, :], x0[PAD + 1 : PAD + 1 + n, :])
    )

    group = iota((PITCH, 256), 0)
    inside = jnp.where(
        group == 0, has_left, jnp.where(group >= 33, has_right, 1.0)
    )[None]

    def finish(ref, value, outer):
        rows = value.shape[0] // PITCH
        kept = jnp.maximum(value, 0.0).reshape(rows, PITCH, 256) * inside
        ref[PAD : PAD + rows * PITCH, :] = (
            kept.reshape(rows * PITCH, 256).astype(BF16).astype(F32)
        )

        @pl.when(top)
        def _():
            ref[PAD : PAD + outer * PITCH, :] = jnp.zeros((outer * PITCH, 256), F32)

        @pl.when(bottom)
        def _():
            ref[PAD + (rows - outer) * PITCH : PAD + rows * PITCH, :] = jnp.zeros(
                (outer * PITCH, 256), F32
            )

    m = 22 * PITCH
    wide = jnp.concatenate(
        [x1[PITCH * dy : PITCH * dy + m, :].astype(BF16) for dy in range(3)], axis=1
    )
    finish(e1, mm(wide, w1[...]), 3)

    def convolve(ref, layer, rows_in):
        n = rows_in * PITCH
        m = (rows_in - 2) * PITCH
        lane = iota((n, 128), 1)
        beside = jnp.where(
            lane < 64, ref[PAD + 1 : PAD + 1 + n, 0:128], ref[PAD - 1 : PAD - 1 + n, 128:256]
        )
        edge[0:n, :] = beside
        outer = (iota((m, 128), 1) < 32) | (iota((m, 128), 1) >= 96)
        between = pltpu.roll(beside, 64, 1)[PITCH : PITCH + m, :]
        wide = jnp.concatenate(
            [ref[PAD + PITCH * dy : PAD + PITCH * dy + m, :].astype(BF16) for dy in range(3)]
            + [
                jnp.where(outer, edge[0:m, :], between).astype(BF16),
                edge[2 * PITCH : 2 * PITCH + m, :].astype(BF16),
            ],
            axis=1,
        )
        return mm(wide, wb[layer])

    finish(e2, convolve(e1, 0, 22), 2)
    finish(d1, convolve(e2, 1, 20), 1)
    m = 16 * PITCH
    d2 = jnp.maximum(convolve(d1, 2, 18) + e1[PAD + 3 * PITCH : PAD + 3 * PITCH + m, :], 0.0)
    projected = mm(d2.astype(BF16), wo[...])
    for c in range(3):
        fo[c] = projected[:, 128 * c : 128 * c + 128]
    of_group = iota((16, 128), 1) // 8
    for c in range(3):
        for half in range(2):
            found = jnp.zeros((16, 128), F32)
            for g in range(16):
                rows = pl.ds(1 + 16 * half + g, 16, stride=PITCH)
                found = jnp.where(of_group == g, fo[c, rows, :], found)
            there = slice(128 * half, 128 * half + 128)
            out[c, :, there] = (found + base[c, :, there]).astype(BF16)


def kernel(
    n_slab,
    n_tile,
    *refs,
):
    inputs, staged = refs[:11], refs[12:23]
    out, load, refs = refs[11], refs[23], refs[24:]
    loads = [
        pltpu.make_async_copy(src, dst, load.at[n])
        for n, (src, dst) in enumerate(zip(inputs, staged))
    ]
    run(n_slab, n_tile, loads, *staged, out, *refs)


def run(
    n_slab,
    n_tile,
    loads,
    density,
    color,
    brick_row,
    brick_col,
    steps,
    flip,
    w_in,
    w_enc,
    w_dec,
    w_dec2,
    w_out,
    out,
    part,
    place,
    canvas_of,
    a_out,
    a_in,
    am_out,
    am_land,
    am_in,
    canvas,
    b_out,
    b_in,
    bm_out,
    bm_in,
    tint,
    h_own,
    h_edge,
    h_rows,
    h_sides,
    ext,
    x0,
    x1,
    e1,
    e2,
    d1,
    edge,
    w1,
    wb,
    wo,
    fo,
    base,
    am_send,
    am_recv,
    a_send,
    a_recv,
    bm_send,
    bm_recv,
    b_send,
    b_recv,
    h_send,
    h_recv,
):
    s = lax.axis_index("slab")
    t = lax.axis_index("tile")
    bricks = density.shape[0]
    slots = CAP * n_tile
    owned = 64 * n_slab

    def tile_peer(i):
        return (s, lax.rem(t + i, n_tile))

    def slab_peer(j):
        return (lax.rem(s + j, n_slab), t)

    def near(ds, dt):
        return (lax.rem(s + ds + n_slab, n_slab), lax.rem(t + dt + n_tile, n_tile))

    corners = [near(-1, -1), near(-1, 1), near(1, -1), near(1, 1)]
    greeted = (
        [tile_peer(i) for i in range(1, n_tile)]
        + [slab_peer(j) for j in range(1, n_slab)]
        + corners
    )
    barrier = pltpu.get_barrier_semaphore()
    for peer in greeted:
        pl.semaphore_signal(barrier, inc=1, device_id=peer, device_id_type=MESH)

    for n in (3, 2, 1, 0, 4, 5, 6, 7, 8, 9, 10):
        loads[n].start()
    for n in (1, 2, 3):
        loads[n].wait()
    col = brick_col[...]
    row = brick_row[...]
    rel = (col // 32 - t + n_tile) % n_tile
    mine = iota((n_tile, bricks), 0) == rel
    before = as_bf16(iota((bricks, bricks), 0) < iota((bricks, bricks), 1))
    ahead = mm(as_bf16(mine), before)
    rank = jnp.sum(jnp.where(mine, ahead, 0.0), axis=0, keepdims=True).astype(jnp.int32)
    slot = rel * CAP + rank
    place[...] = as_bf16(iota((slots, bricks), 0) == slot)
    block = (row // 2 - s + n_slab) % n_slab
    tile_id = (block * 64 + row % 2 * 32 + col % 32 + 1).astype(F32)
    in_slot = iota((CAP, bricks), 0) == rank
    tints = color[...]
    fields = [tints[0:1, :], tints[1:2, :], tints[2:3, :], tile_id]
    spread = jnp.concatenate([jnp.where(in_slot, f, 0.0) for f in fields], axis=0)
    high = spread.astype(BF16)
    low = (spread - high.astype(F32)).astype(BF16)
    owner = as_bf16(mine)
    notes = mm_nt(owner, high) + mm_nt(owner, low)
    for i in range(1, n_tile):
        am_out[i] = notes[i : i + 1, :]
    am_in[0:1, :] = notes[0:1, :]

    def start(src, dst, send, recv, peer):
        copy = pltpu.make_async_remote_copy(
            src_ref=src,
            dst_ref=dst,
            send_sem=send,
            recv_sem=recv,
            device_id=peer,
            device_id_type=MESH,
        )
        copy.start()
        return copy

    loads[0].wait()
    loads[4].wait()
    ray_march(density, steps, part)
    for g in range(slots // 128):
        a_out[128 * g : 128 * g + 128, :] = join(
            mm(place[128 * g : 128 * g + 128, :], part[...])
        )
    a_in[0:CAP, :] = a_out[0:CAP, :]

    pl.semaphore_wait(barrier, len(greeted))
    across = range(1, n_tile)
    am_copies = {
        i: start(am_out.at[i], am_land.at[i], am_send.at[i], am_recv.at[i], tile_peer(i))
        for i in across
    }
    a_copies = {}
    for i in across:
        span = pl.ds(CAP * i, CAP)
        a_copies[i] = start(
            a_out.at[span], a_in.at[span], a_send.at[i], a_recv.at[i], tile_peer(i)
        )

    for n in (6, 7, 8, 9, 10):
        loads[n].wait()
    build_weights(w_in, (w_enc, w_dec, w_dec2), w_out, w1, wb, wo)
    ext[...] = jnp.zeros(ext.shape, F32)
    for ref in (x0, e1, e2, d1):
        width = ref.shape[1]
        ref[0:PAD, :] = jnp.zeros((PAD, width), F32)
        ref[ref.shape[0] - PAD :, :] = jnp.zeros((PAD, width), F32)

    for i in range(1, n_tile):
        am_copies[i].wait_recv()
        am_in[i : i + 1, :] = am_land[i]
    notes = am_in[...]
    high = notes.astype(BF16)
    both = jnp.concatenate([high, (notes - high.astype(F32)).astype(BF16)], axis=0)
    from_peer = iota((2 * n_tile, slots), 0) % n_tile == iota((2 * n_tile, slots), 1) // CAP
    in_row = iota((128, slots), 0) - iota((128, slots), 1) % CAP
    field = iota((16, slots), 0)
    arrived = jnp.zeros((16, slots), F32)
    for f in range(4):
        here = jnp.where(from_peer, mm(both, as_bf16(in_row == CAP * f)), 0.0)
        high = jnp.sum(here[0:n_tile], axis=0, keepdims=True)
        low = jnp.sum(here[n_tile:], axis=0, keepdims=True)
        if f < 3:
            arrived = jnp.where(field == 2 * f, high, jnp.where(field == 2 * f + 1, low, arrived))
        else:
            tile_id = (high + low).astype(jnp.int32) - 1
            arrived = jnp.where((field == 8) & (tile_id >= 0), 1.0, arrived)
    canvas_of[...] = as_bf16(iota((owned, slots), 0) == tile_id)
    tile_meta = mm_nt(arrived.astype(BF16), canvas_of[...]).astype(BF16)
    for g in range(n_slab // 2):
        bm_out[g] = tile_meta[:, 128 * g : 128 * g + 128]
    bm_in[0] = bm_out[0]
    bm_copies = [
        start(bm_out.at[j // 2], bm_in.at[j], bm_send.at[j], bm_recv.at[j], slab_peer(j))
        for j in range(1, n_slab)
    ]

    chunk = min(256, slots)
    spans = [slice(k * chunk, (k + 1) * chunk) for k in (0, 1, 3, 2) if k * chunk < slots]
    for k, span in enumerate(spans):
        for i in range(max(1, span.start // CAP), span.stop // CAP):
            a_copies[i].wait_recv()
        came = split(a_in[span, :].astype(jnp.int32) + 32768)
        if k + 1 < len(spans):
            term = mm(canvas_of[:, span], came)
            if k == 0:
                canvas[...] = term
            else:
                canvas[...] += term
    b_copies = []
    for pair in range(n_slab // 2):
        rows = slice(128 * pair, 128 * pair + 128)
        levels = mm(canvas_of[rows, span], came)
        if len(spans) > 1:
            levels = levels + canvas[rows, :]
        levels = join(levels)
        for j in (2 * pair, 2 * pair + 1):
            piece = levels[64 * (j % 2) : 64 * (j % 2) + 64, :]
            if j == 0:
                b_in[0] = piece
            else:
                b_out[j] = piece
                b_copies.append(
                    start(b_out.at[j], b_in.at[j], b_send.at[j], b_recv.at[j], slab_peer(j))
                )

    for copy in bm_copies:
        copy.wait_recv()
    lane_c = iota((16, 256), 1) // 64
    field = iota((16, 256), 0)
    choose = as_bf16(((field // 2 == lane_c) & (lane_c < 3) & (field < 6)) | ((field == 8) & (lane_c == 3)))
    for j in range(n_slab):
        both = mm_tn(bm_in[j], choose)
        tint[j] = both[64 * (j % 2) : 64 * (j % 2) + 64, :]

    loads[5].wait()
    flips = flip[pl.ds(2 * s, 2), :]
    same = iota((32, 32), 0) == iota((32, 32), 1)
    flipped = (
        jnp.concatenate(
            [
                jnp.sum(jnp.where(same, flips[r : r + 1, :], 0), axis=1, keepdims=True)
                for r in range(2)
            ],
            axis=0,
        )
        == 1
    )

    for copy in b_copies:
        copy.wait_recv()
    front = iota((64, 128), 1) < 64
    scale = scales((64, 128))
    light0 = jnp.zeros((64, 128), F32)
    light1 = jnp.zeros((64, 128), F32)
    trans = jnp.ones((64, 128), F32)
    for k in range(n_slab):
        first = lax.rem(s - k + n_slab, n_slab)
        last = lax.rem(s - (n_slab - 1 - k) + n_slab, n_slab)
        level = jnp.where(
            flipped, b_in[last].astype(jnp.int32), b_in[first].astype(jnp.int32)
        )
        piece = (level + 32768).astype(F32) * scale
        hue = jnp.where(flipped, tint[last], tint[first])
        turned = pltpu.roll(piece, 64, 1)
        part0 = (jnp.where(front, piece, turned) * hue[:, 0:128]).astype(BF16).astype(F32)
        part1 = (piece * hue[:, 128:256]).astype(BF16).astype(F32)
        alpha = jnp.where(front, pltpu.roll(part1, 64, 1), part1)
        light0 = light0 + trans * part0
        light1 = light1 + trans * part1
        trans = trans * (1.0 - alpha)
    composite = jnp.concatenate([light0, light1], axis=1).astype(BF16)
    h_own[...] = composite
    own = composite.astype(F32)
    edge_row = iota((16, 256), 0)
    for side, at in ((0, 0), (1, 31)):
        h_edge[side] = jnp.where(
            edge_row == 0,
            own[at : at + 1, :],
            jnp.where(edge_row == 1, own[at + 32 : at + 33, :], 0.0),
        ).astype(BF16)
    up, down, left, right = near(-1, 0), near(1, 0), near(0, -1), near(0, 1)
    plan = [
        (h_edge.at[0], h_sides.at[5], corners[0]),
        (h_edge.at[1], h_sides.at[4], corners[1]),
        (h_edge.at[0], h_sides.at[3], corners[2]),
        (h_edge.at[1], h_sides.at[2], corners[3]),
        (h_edge.at[0], h_sides.at[1], left),
        (h_edge.at[1], h_sides.at[0], right),
        (h_own.at[pl.ds(0, 32)], h_rows.at[1], up),
        (h_own.at[pl.ds(32, 32)], h_rows.at[0], down),
    ]
    h_copies = [
        start(src, dst, h_send.at[n], h_recv.at[n], peer) for n, (src, dst, peer) in enumerate(plan)
    ]
    has_up = jnp.where(s > 0, 1.0, 0.0)
    has_down = jnp.where(s < n_slab - 1, 1.0, 0.0)
    has_left = jnp.where(t > 0, 1.0, 0.0)
    has_right = jnp.where(t < n_tile - 1, 1.0, 0.0)
    ext[PITCH + 1 : PITCH + 33, :] = own[0:32, :]
    ext[2 * PITCH + 1 : 2 * PITCH + 33, :] = own[32:64, :]
    lay_out(composite, base)
    for copy in h_copies:
        copy.wait_recv()
    ext[1:33, :] = h_rows[0].astype(F32) * has_up
    ext[3 * PITCH + 1 : 3 * PITCH + 33, :] = h_rows[1].astype(F32) * has_down
    sides = [
        (0, has_left, ((PITCH, 0), (2 * PITCH, 1))),
        (1, has_right, ((PITCH + 33, 0), (2 * PITCH + 33, 1))),
        (2, has_up * has_left, ((0, 1),)),
        (3, has_up * has_right, ((33, 1),)),
        (4, has_down * has_left, ((3 * PITCH, 0),)),
        (5, has_down * has_right, ((3 * PITCH + 33, 0),)),
    ]
    for n, there, moves in sides:
        block = h_sides[n].astype(F32) * there
        for at, r in moves:
            ext[at : at + 1, :] = block[r : r + 1, :]

    denoise(
        s == 0, s == n_slab - 1, has_left, has_right, ext, x0, x1, e1, e2, d1, edge, w1, wb, wo, fo, base, out
    )

    for copy in [*am_copies.values(), *a_copies.values()] + bm_copies + b_copies + h_copies:
        copy.wait_send()


def shards(
    density,
    brick_color,
    brick_row,
    brick_col,
    brick_steps,
    depth_flip,
    w_in,
    w_enc,
    w_dec,
    w_dec2,
    w_out,
):
    n_tile = lax.axis_size("tile")
    n_slab = lax.axis_size("slab")
    bricks = density.shape[0]
    slots = CAP * n_tile
    owned = 64 * n_slab
    taps = [jnp.transpose(w, (2, 3, 0, 1)).reshape(288, 32) for w in (w_enc, w_dec, w_dec2)]
    vmem = pl.BlockSpec(memory_space=pltpu.VMEM)
    dma = pltpu.SemaphoreType.DMA
    operands = (
        density,
        brick_color,
        brick_row.reshape(1, bricks),
        brick_col.reshape(1, bricks),
        brick_steps.reshape(1, bricks),
        depth_flip,
        jnp.transpose(w_in, (2, 3, 1, 0)).reshape(9, 4, 32),
        *taps,
        w_out,
    )
    return pl.pallas_call(
        functools.partial(kernel, n_slab, n_tile),
        out_shape=jax.ShapeDtypeStruct((3, 16, 256), BF16),
        in_specs=[pl.BlockSpec(memory_space=pltpu.HBM)] * 11,
        out_specs=vmem,
        scratch_shapes=[pltpu.VMEM(x.shape, x.dtype) for x in operands]
        + [
            dma((11,)),
            pltpu.VMEM((bricks, 256), BF16),
            pltpu.VMEM((slots, bricks), BF16),
            pltpu.VMEM((owned, slots), BF16),
            pltpu.VMEM((slots, 128), jnp.int16),
            pltpu.VMEM((slots, 128), jnp.int16),
            pltpu.VMEM((n_tile, 1, 128), F32),
            pltpu.VMEM((n_tile, 1, 128), F32),
            pltpu.VMEM((n_tile, 128), F32),
            pltpu.VMEM((owned, 256), F32),
            pltpu.VMEM((n_slab, 64, 128), jnp.int16),
            pltpu.VMEM((n_slab, 64, 128), jnp.int16),
            pltpu.VMEM((n_slab // 2, 16, 128), BF16),
            pltpu.VMEM((n_slab, 16, 128), BF16),
            pltpu.VMEM((n_slab, 64, 256), F32),
            pltpu.VMEM((64, 256), BF16),
            pltpu.VMEM((2, 16, 256), BF16),
            pltpu.VMEM((2, 32, 256), BF16),
            pltpu.VMEM((6, 16, 256), BF16),
            pltpu.VMEM((4 * PITCH, 256), F32),
            pltpu.VMEM((24 * PITCH + 2 * PAD, 128), F32),
            pltpu.VMEM((24 * PITCH, 128), F32),
            pltpu.VMEM((22 * PITCH + 2 * PAD, 256), F32),
            pltpu.VMEM((20 * PITCH + 2 * PAD, 256), F32),
            pltpu.VMEM((18 * PITCH + 2 * PAD, 256), F32),
            pltpu.VMEM((22 * PITCH, 128), F32),
            pltpu.VMEM((384, 256), BF16),
            pltpu.VMEM((3, 1024, 256), BF16),
            pltpu.VMEM((256, 384), BF16),
            pltpu.VMEM((3, 16 * PITCH, 128), F32),
            pltpu.VMEM((3, 16, 256), F32),
            dma((n_tile,)),
            dma((n_tile,)),
            dma((n_tile,)),
            dma((n_tile,)),
            dma((n_slab,)),
            dma((n_slab,)),
            dma((n_slab,)),
            dma((n_slab,)),
            dma((8,)),
            dma((8,)),
        ],
        compiler_params=pltpu.CompilerParams(
            collective_id=0, has_side_effects=True, vmem_limit_bytes=62 * 1024 * 1024
        ),
    )(*operands)


def solution(mesh):
    return jax.shard_map(
        shards,
        mesh=mesh,
        in_specs=(
            P(("slab", "tile"), None),
            P(None, ("slab", "tile")),
            P(("slab", "tile")),
            P(("slab", "tile")),
            P(("slab", "tile")),
            P(None, "tile"),
            P(),
            P(),
            P(),
            P(),
            P(),
        ),
        out_specs=P(None, "slab", "tile"),
        check_vma=False,
    )
```

```python
import functools
import jax
import jax.numpy as jnp
from jax import lax
from jax.experimental import pallas as pl
from jax.experimental.pallas import tpu as pltpu
from jax.sharding import PartitionSpec as P

MESH = pl.DeviceIdType.MESH
BF16 = jnp.bfloat16
F32 = jnp.float32
STEP = 0.03
CAP = 32
PITCH = 40
PAD = 8
LIGHT_TOP = 2.5
ALPHA_TOP = 0.625
LEVELS = 65535.0


def iota(shape, dim):
    return lax.broadcasted_iota(jnp.int32, shape, dim)


def as_bf16(cond):
    return jnp.where(cond, 1.0, 0.0).astype(BF16)


def mm(a, b):
    return jnp.dot(a, b, preferred_element_type=F32)


def mm_nt(a, b):
    return lax.dot_general(a, b, (((1,), (1,)), ((), ())), preferred_element_type=F32)


def mm_tn(a, b):
    return lax.dot_general(a, b, (((0,), (0,)), ((), ())), preferred_element_type=F32)


def scales(shape):
    front = iota(shape, 1) < 64
    return jnp.where(front, LIGHT_TOP / LEVELS, ALPHA_TOP / LEVELS)


def split(levels):
    high = levels // 256
    low = levels - 256 * high
    return jnp.concatenate([high.astype(F32), low.astype(F32)], axis=1).astype(BF16)


def join(halves):
    levels = (256.0 * halves[:, 0:128] + halves[:, 128:256]).astype(jnp.int32)
    return (levels - 32768).astype(jnp.int16)


def build_weights(w_in, w_layers, w_out, w1, wb, wo):
    spread = as_bf16(iota((32, 256), 0) == iota((32, 256), 1) % 32)
    lane_x = iota((32, 256), 1) // 32
    for layer, w_ref in enumerate(w_layers):
        turned = jnp.transpose(w_ref[...].astype(F32))
        for ky in range(3):
            taps = [
                mm(turned[:, 32 * (3 * ky + kx) : 32 * (3 * ky + kx) + 32].astype(BF16), spread)
                for kx in range(3)
            ]
            base = 256 * ky
            for x_in in range(8):
                total = jnp.zeros((32, 256), F32)
                for kx in range(3):
                    total = jnp.where(lane_x == x_in - kx + 1, taps[kx], total)
                wb[layer, base + 32 * x_in : base + 32 * x_in + 32, :] = total.astype(BF16)
            right, left = ((768, 864), (832, 800), (896, 992))[ky]
            wb[layer, right : right + 32, :] = jnp.where(lane_x == 7, taps[2], 0.0).astype(BF16)
            wb[layer, left : left + 32, :] = jnp.where(lane_x == 0, taps[0], 0.0).astype(BF16)
        wb[layer, 928:992, :] = jnp.zeros((64, 256), BF16)
    row = iota((128, 256), 0)
    lane_x = iota((128, 256), 1) // 32
    third = row // 32
    x_in = (row % 32) // 4 + jnp.where(third == 1, -8, jnp.where(third == 2, 8, 0))
    pick = as_bf16((iota((128, 4), 0) % 4 == iota((128, 4), 1)) & (iota((128, 4), 0) < 96))
    for ky in range(3):
        total = jnp.zeros((128, 256), F32)
        for kx in range(3):
            tap = mm(mm(pick, w_in[3 * ky + kx]).astype(BF16), spread)
            total = jnp.where(lane_x == x_in - kx + 1, tap, total)
        w1[128 * ky : 128 * ky + 128, :] = total.astype(BF16)
    spread_t = as_bf16(iota((256, 32), 1) == iota((256, 32), 0) % 32)
    same_x = iota((256, 128), 0) // 32 == iota((256, 128), 1) % 8
    for c in range(3):
        along = mm_nt(spread_t, jnp.broadcast_to(w_out[c : c + 1, :], (128, 32)))
        wo[0:256, 128 * c : 128 * c + 128] = jnp.where(same_x, along, 0.0).astype(BF16)


def ray_march(density, steps, part):
    lane = iota((64, 128), 1)
    front = lane < 64
    half = jnp.where(front, 0, 1)
    for chunk in range(density.shape[0] // 64):
        rows = slice(64 * chunk, 64 * chunk + 64)
        group = steps[:, 128 * (64 * chunk // 128) : 128 * (64 * chunk // 128) + 128].astype(F32)
        off = (64 * chunk) % 128
        eye = iota((64, 128), 0) + off == iota((64, 128), 1)
        alive = mm(jnp.where(eye, group, 0.0).astype(BF16), jnp.ones((128, 128), BF16))
        alive = alive.astype(jnp.int32)
        light = jnp.zeros((64, 128), F32)
        trans = jnp.ones((64, 128), F32)
        for j in range(4):
            sigma = density[rows, 128 * j : 128 * j + 128].astype(F32)
            keep = jnp.where(half + 2 * j < alive, jnp.exp(-STEP * sigma), 1.0)
            emit = (1.0 - keep) * sigma
            other = pltpu.roll(keep, 64, 1)
            light = light + trans * jnp.where(front, 1.0, other) * emit
            trans = trans * (keep * other)
        light = light + pltpu.roll(light, 64, 1)
        value = jnp.where(
            front, light * (LEVELS / LIGHT_TOP), (1.0 - trans) * (LEVELS / ALPHA_TOP)
        )
        part[rows, :] = split((value + 0.5).astype(jnp.int32))


def lay_out(tiles, base):
    row = iota((256, 384), 0)
    lane = iota((256, 384), 1)
    source = lane // 128 * 64 + lane % 8
    of_tile = iota((16, 128), 0) == iota((16, 128), 1) // 8
    for y in range(8):
        spread = mm(tiles, as_bf16(row == source + 8 * y))
        for tr in range(2):
            for half in range(2):
                first = 32 * tr + 16 * half
                for c in range(3):
                    block = spread[first : first + 16, 128 * c : 128 * c + 128]
                    base[c, 8 * tr + y : 8 * tr + y + 1, 128 * half : 128 * half + 128] = jnp.sum(
                        jnp.where(of_tile, block, 0.0), axis=0, keepdims=True
                    )


def denoise(
    top, bottom, has_left, has_right, ext, x0, x1, e1, e2, d1, edge, w1, wb, wo, fo, base, out
):
    tiles = ext[...].astype(BF16)
    lane = iota((256, 128), 1)
    source = (lane % 4) * 64 + (lane % 32) // 4
    for y in range(8):
        turn = as_bf16((iota((256, 128), 0) == source + 8 * y) & (lane < 96))
        rows = mm(tiles, turn)
        for tr in range(4):
            r = 8 * tr + y - 4
            if 0 <= r < 24:
                x0[PAD + PITCH * r : PAD + PITCH * r + PITCH, :] = rows[
                    PITCH * tr : PITCH * tr + PITCH, :
                ]
    n = 24 * PITCH
    lane = iota((n, 128), 1)
    x1[...] = jnp.where(
        lane < 32, x0[PAD : PAD + n, :], jnp.where(lane < 64, x0[PAD - 1 : PAD - 1 + n, :], x0[PAD + 1 : PAD + 1 + n, :])
    )

    group = iota((PITCH, 256), 0)
    inside = jnp.where(
        group == 0, has_left, jnp.where(group >= 33, has_right, 1.0)
    )[None]

    def finish(ref, value, outer):
        rows = value.shape[0] // PITCH
        kept = jnp.maximum(value, 0.0).reshape(rows, PITCH, 256) * inside
        ref[PAD : PAD + rows * PITCH, :] = (
            kept.reshape(rows * PITCH, 256).astype(BF16).astype(F32)
        )

        @pl.when(top)
        def _():
            ref[PAD : PAD + outer * PITCH, :] = jnp.zeros((outer * PITCH, 256), F32)

        @pl.when(bottom)
        def _():
            ref[PAD + (rows - outer) * PITCH : PAD + rows * PITCH, :] = jnp.zeros(
                (outer * PITCH, 256), F32
            )

    m = 22 * PITCH
    wide = jnp.concatenate(
        [x1[PITCH * dy : PITCH * dy + m, :].astype(BF16) for dy in range(3)], axis=1
    )
    finish(e1, mm(wide, w1[...]), 3)

    def convolve(ref, layer, rows_in):
        n = rows_in * PITCH
        m = (rows_in - 2) * PITCH
        lane = iota((n, 128), 1)
        beside = jnp.where(
            lane < 64, ref[PAD + 1 : PAD + 1 + n, 0:128], ref[PAD - 1 : PAD - 1 + n, 128:256]
        )
        edge[0:n, :] = beside
        outer = (iota((m, 128), 1) < 32) | (iota((m, 128), 1) >= 96)
        between = pltpu.roll(beside, 64, 1)[PITCH : PITCH + m, :]
        wide = jnp.concatenate(
            [ref[PAD + PITCH * dy : PAD + PITCH * dy + m, :].astype(BF16) for dy in range(3)]
            + [
                jnp.where(outer, edge[0:m, :], between).astype(BF16),
                edge[2 * PITCH : 2 * PITCH + m, :].astype(BF16),
            ],
            axis=1,
        )
        return mm(wide, wb[layer])

    finish(e2, convolve(e1, 0, 22), 2)
    finish(d1, convolve(e2, 1, 20), 1)
    m = 16 * PITCH
    d2 = jnp.maximum(convolve(d1, 2, 18) + e1[PAD + 3 * PITCH : PAD + 3 * PITCH + m, :], 0.0)
    projected = mm(d2.astype(BF16), wo[...])
    for c in range(3):
        fo[c, 0:m, :] = projected[:, 128 * c : 128 * c + 128]
    of_group = iota((16, 128), 1) // 8
    for c in range(3):
        for half in range(2):
            found = jnp.zeros((16, 128), F32)
            for g in range(16):
                rows = pl.ds(1 + 16 * half + g, 16, stride=PITCH)
                found = jnp.where(of_group == g, fo[c, rows, :], found)
            there = slice(128 * half, 128 * half + 128)
            out[c, :, there] = (found + base[c, :, there]).astype(BF16)


def kernel(
    n_slab,
    n_tile,
    *refs,
):
    inputs, staged = refs[:11], refs[12:23]
    out, load, refs = refs[11], refs[23], refs[24:]
    loads = [
        pltpu.make_async_copy(src, dst, load.at[n])
        for n, (src, dst) in enumerate(zip(inputs, staged))
    ]
    run(n_slab, n_tile, loads, *staged, out, *refs)


def run(
    n_slab,
    n_tile,
    loads,
    density,
    color,
    brick_row,
    brick_col,
    steps,
    flip,
    w_in,
    w_enc,
    w_dec,
    w_dec2,
    w_out,
    out,
    part,
    place,
    canvas_of,
    a_out,
    a_in,
    am_out,
    am_land,
    am_in,
    canvas,
    b_out,
    b_in,
    bm_out,
    bm_in,
    tint,
    h_own,
    h_edge,
    h_rows,
    h_sides,
    ext,
    x0,
    x1,
    e1,
    e2,
    d1,
    edge,
    w1,
    wb,
    wo,
    fo,
    base,
    am_send,
    am_recv,
    a_send,
    a_recv,
    bm_send,
    bm_recv,
    b_send,
    b_recv,
    h_send,
    h_recv,
):
    s = lax.axis_index("slab")
    t = lax.axis_index("tile")
    bricks = density.shape[0]
    slots = CAP * n_tile
    owned = 64 * n_slab

    def tile_peer(i):
        return (s, lax.rem(t + i, n_tile))

    def slab_peer(j):
        return (lax.rem(s + j, n_slab), t)

    def near(ds, dt):
        return (lax.rem(s + ds + n_slab, n_slab), lax.rem(t + dt + n_tile, n_tile))

    corners = [near(-1, -1), near(-1, 1), near(1, -1), near(1, 1)]
    greeted = (
        corners
        + [slab_peer(j) for j in range(1, n_slab)]
        + [tile_peer(i) for i in range(1, n_tile)]
    )
    barrier = pltpu.get_barrier_semaphore()
    for peer in greeted:
        pl.semaphore_signal(barrier, inc=1, device_id=peer, device_id_type=MESH)

    for n in (3, 2, 1, 0, 4, 5, 6, 7, 8, 9, 10):
        loads[n].start()
    for n in (1, 2, 3):
        loads[n].wait()
    col = brick_col[...]
    row = brick_row[...]
    rel = (col // 32 - t + n_tile) % n_tile
    mine = iota((n_tile, bricks), 0) == rel
    before = as_bf16(iota((bricks, bricks), 0) < iota((bricks, bricks), 1))
    ahead = mm(as_bf16(mine), before)
    rank = jnp.sum(jnp.where(mine, ahead, 0.0), axis=0, keepdims=True).astype(jnp.int32)
    slot = rel * CAP + rank
    place[...] = as_bf16(iota((slots, bricks), 0) == slot)
    block = (row // 2 - s + n_slab) % n_slab
    tile_id = (block * 64 + row % 2 * 32 + col % 32 + 1).astype(F32)
    in_slot = iota((CAP, bricks), 0) == rank
    tints = color[...]
    fields = [tints[0:1, :], tints[1:2, :], tints[2:3, :], tile_id]
    spread = jnp.concatenate([jnp.where(in_slot, f, 0.0) for f in fields], axis=0)
    high = spread.astype(BF16)
    low = (spread - high.astype(F32)).astype(BF16)
    owner = as_bf16(mine)
    notes = mm_nt(owner, high) + mm_nt(owner, low)
    for i in range(1, n_tile):
        am_out[i] = notes[i : i + 1, :]
    am_in[0:1, :] = notes[0:1, :]

    def start(src, dst, send, recv, peer):
        copy = pltpu.make_async_remote_copy(
            src_ref=src,
            dst_ref=dst,
            send_sem=send,
            recv_sem=recv,
            device_id=peer,
            device_id_type=MESH,
        )
        copy.start()
        return copy

    loads[0].wait()
    loads[4].wait()
    ray_march(density, steps, part)
    for g in range(slots // 128):
        a_out[128 * g : 128 * g + 128, :] = join(
            mm(place[128 * g : 128 * g + 128, :], part[...])
        )
    a_in[0:CAP, :] = a_out[0:CAP, :]

    pl.semaphore_wait(barrier, len(greeted))
    across = range(1, n_tile)
    am_copies = {
        i: start(am_out.at[i], am_land.at[i], am_send.at[i], am_recv.at[i], tile_peer(i))
        for i in across
    }
    a_copies = {}
    for i in across:
        span = pl.ds(CAP * i, CAP)
        a_copies[i] = start(
            a_out.at[span], a_in.at[span], a_send.at[i], a_recv.at[i], tile_peer(i)
        )

    for n in (6, 7, 8, 9, 10):
        loads[n].wait()
    build_weights(w_in, (w_enc, w_dec, w_dec2), w_out, w1, wb, wo)
    ext[...] = jnp.zeros(ext.shape, F32)
    for ref in (x0, e1, e2, d1):
        width = ref.shape[1]
        ref[0:PAD, :] = jnp.zeros((PAD, width), F32)
        ref[ref.shape[0] - PAD :, :] = jnp.zeros((PAD, width), F32)

    for i in range(1, n_tile):
        am_copies[i].wait_recv()
        am_in[i : i + 1, :] = am_land[i]
    notes = am_in[...]
    high = notes.astype(BF16)
    both = jnp.concatenate([high, (notes - high.astype(F32)).astype(BF16)], axis=0)
    from_peer = iota((2 * n_tile, slots), 0) % n_tile == iota((2 * n_tile, slots), 1) // CAP
    in_row = iota((128, slots), 0) - iota((128, slots), 1) % CAP
    field = iota((16, slots), 0)
    arrived = jnp.zeros((16, slots), F32)
    for f in range(4):
        here = jnp.where(from_peer, mm(both, as_bf16(in_row == CAP * f)), 0.0)
        high = jnp.sum(here[0:n_tile], axis=0, keepdims=True)
        low = jnp.sum(here[n_tile:], axis=0, keepdims=True)
        if f < 3:
            arrived = jnp.where(field == 2 * f, high, jnp.where(field == 2 * f + 1, low, arrived))
        else:
            tile_id = (high + low).astype(jnp.int32) - 1
            arrived = jnp.where((field == 8) & (tile_id >= 0), 1.0, arrived)
    canvas_of[...] = as_bf16(iota((owned, slots), 0) == tile_id)
    tile_meta = mm_nt(arrived.astype(BF16), canvas_of[...]).astype(BF16)
    for g in range(n_slab // 2):
        bm_out[g] = tile_meta[:, 128 * g : 128 * g + 128]
    bm_in[0] = bm_out[0]
    bm_copies = [
        start(bm_out.at[j // 2], bm_in.at[j], bm_send.at[j], bm_recv.at[j], slab_peer(j))
        for j in range(1, n_slab)
    ]

    chunk = min(256, slots)
    spans = [slice(k * chunk, (k + 1) * chunk) for k in (0, 1, 3, 2) if k * chunk < slots]
    for k, span in enumerate(spans):
        for i in range(max(1, span.start // CAP), span.stop // CAP):
            a_copies[i].wait_recv()
        came = split(a_in[span, :].astype(jnp.int32) + 32768)
        if k + 1 < len(spans):
            term = mm(canvas_of[:, span], came)
            if k == 0:
                canvas[...] = term
            else:
                canvas[...] += term
    b_copies = []
    for pair in range(n_slab // 2):
        rows = slice(128 * pair, 128 * pair + 128)
        levels = mm(canvas_of[rows, span], came)
        if len(spans) > 1:
            levels = levels + canvas[rows, :]
        levels = join(levels)
        for j in (2 * pair, 2 * pair + 1):
            piece = levels[64 * (j % 2) : 64 * (j % 2) + 64, :]
            if j == 0:
                b_in[0] = piece
            else:
                b_out[j] = piece
                b_copies.append(
                    start(b_out.at[j], b_in.at[j], b_send.at[j], b_recv.at[j], slab_peer(j))
                )

    for copy in bm_copies:
        copy.wait_recv()
    lane_c = iota((16, 256), 1) // 64
    field = iota((16, 256), 0)
    choose = as_bf16(((field // 2 == lane_c) & (lane_c < 3) & (field < 6)) | ((field == 8) & (lane_c == 3)))
    for j in range(n_slab):
        both = mm_tn(bm_in[j], choose)
        tint[j] = both[64 * (j % 2) : 64 * (j % 2) + 64, :]

    loads[5].wait()
    flips = flip[pl.ds(2 * s, 2), :]
    same = iota((32, 32), 0) == iota((32, 32), 1)
    flipped = (
        jnp.concatenate(
            [
                jnp.sum(jnp.where(same, flips[r : r + 1, :], 0), axis=1, keepdims=True)
                for r in range(2)
            ],
            axis=0,
        )
        == 1
    )

    for copy in b_copies:
        copy.wait_recv()
    front = iota((64, 128), 1) < 64
    scale = scales((64, 128))
    light0 = jnp.zeros((64, 128), F32)
    light1 = jnp.zeros((64, 128), F32)
    trans = jnp.ones((64, 128), F32)
    for k in range(n_slab):
        first = lax.rem(s - k + n_slab, n_slab)
        last = lax.rem(s - (n_slab - 1 - k) + n_slab, n_slab)
        level = jnp.where(
            flipped, b_in[last].astype(jnp.int32), b_in[first].astype(jnp.int32)
        )
        piece = (level + 32768).astype(F32) * scale
        hue = jnp.where(flipped, tint[last], tint[first])
        turned = pltpu.roll(piece, 64, 1)
        part0 = (jnp.where(front, piece, turned) * hue[:, 0:128]).astype(BF16).astype(F32)
        part1 = (piece * hue[:, 128:256]).astype(BF16).astype(F32)
        alpha = jnp.where(front, pltpu.roll(part1, 64, 1), part1)
        light0 = light0 + trans * part0
        light1 = light1 + trans * part1
        trans = trans * (1.0 - alpha)
    composite = jnp.concatenate([light0, light1], axis=1).astype(BF16)
    h_own[...] = composite
    own = composite.astype(F32)
    edge_row = iota((16, 256), 0)
    for side, at in ((0, 0), (1, 31)):
        h_edge[side] = jnp.where(
            edge_row == 0,
            own[at : at + 1, :],
            jnp.where(edge_row == 1, own[at + 32 : at + 33, :], 0.0),
        ).astype(BF16)
    up, down, left, right = near(-1, 0), near(1, 0), near(0, -1), near(0, 1)
    plan = [
        (h_edge.at[0], h_sides.at[5], corners[0]),
        (h_edge.at[1], h_sides.at[4], corners[1]),
        (h_edge.at[0], h_sides.at[3], corners[2]),
        (h_edge.at[1], h_sides.at[2], corners[3]),
        (h_edge.at[0], h_sides.at[1], left),
        (h_edge.at[1], h_sides.at[0], right),
        (h_own.at[pl.ds(0, 32)], h_rows.at[1], up),
        (h_own.at[pl.ds(32, 32)], h_rows.at[0], down),
    ]
    h_copies = [
        start(src, dst, h_send.at[n], h_recv.at[n], peer) for n, (src, dst, peer) in enumerate(plan)
    ]
    has_up = jnp.where(s > 0, 1.0, 0.0)
    has_down = jnp.where(s < n_slab - 1, 1.0, 0.0)
    has_left = jnp.where(t > 0, 1.0, 0.0)
    has_right = jnp.where(t < n_tile - 1, 1.0, 0.0)
    ext[PITCH + 1 : PITCH + 33, :] = own[0:32, :]
    ext[2 * PITCH + 1 : 2 * PITCH + 33, :] = own[32:64, :]
    lay_out(composite, base)
    for copy in h_copies:
        copy.wait_recv()
    ext[1:33, :] = h_rows[0].astype(F32) * has_up
    ext[3 * PITCH + 1 : 3 * PITCH + 33, :] = h_rows[1].astype(F32) * has_down
    sides = [
        (0, has_left, ((PITCH, 0), (2 * PITCH, 1))),
        (1, has_right, ((PITCH + 33, 0), (2 * PITCH + 33, 1))),
        (2, has_up * has_left, ((0, 1),)),
        (3, has_up * has_right, ((33, 1),)),
        (4, has_down * has_left, ((3 * PITCH, 0),)),
        (5, has_down * has_right, ((3 * PITCH + 33, 0),)),
    ]
    for n, there, moves in sides:
        block = h_sides[n].astype(F32) * there
        for at, r in moves:
            ext[at : at + 1, :] = block[r : r + 1, :]

    denoise(
        s == 0, s == n_slab - 1, has_left, has_right, ext, x0, x1, e1, e2, d1, edge, w1, wb, wo, fo, base, out
    )

    for copy in [*am_copies.values(), *a_copies.values()] + bm_copies + b_copies + h_copies:
        copy.wait_send()


def shards(
    density,
    brick_color,
    brick_row,
    brick_col,
    brick_steps,
    depth_flip,
    w_in,
    w_enc,
    w_dec,
    w_dec2,
    w_out,
):
    n_tile = lax.axis_size("tile")
    n_slab = lax.axis_size("slab")
    bricks = density.shape[0]
    slots = CAP * n_tile
    owned = 64 * n_slab
    taps = [jnp.transpose(w, (2, 3, 0, 1)).reshape(288, 32) for w in (w_enc, w_dec, w_dec2)]
    vmem = pl.BlockSpec(memory_space=pltpu.VMEM)
    dma = pltpu.SemaphoreType.DMA
    operands = (
        density,
        brick_color,
        brick_row.reshape(1, bricks),
        brick_col.reshape(1, bricks),
        brick_steps.reshape(1, bricks),
        depth_flip,
        jnp.transpose(w_in, (2, 3, 1, 0)).reshape(9, 4, 32),
        *taps,
        w_out,
    )
    return pl.pallas_call(
        functools.partial(kernel, n_slab, n_tile),
        out_shape=jax.ShapeDtypeStruct((3, 16, 256), BF16),
        in_specs=[pl.BlockSpec(memory_space=pltpu.HBM)] * 11,
        out_specs=vmem,
        scratch_shapes=[pltpu.VMEM(x.shape, x.dtype) for x in operands]
        + [
            dma((11,)),
            pltpu.VMEM((bricks, 256), BF16),
            pltpu.VMEM((slots, bricks), BF16),
            pltpu.VMEM((owned, slots), BF16),
            pltpu.VMEM((slots, 128), jnp.int16),
            pltpu.VMEM((slots, 128), jnp.int16),
            pltpu.VMEM((n_tile, 1, 128), F32),
            pltpu.VMEM((n_tile, 1, 128), F32),
            pltpu.VMEM((n_tile, 128), F32),
            pltpu.VMEM((owned, 256), F32),
            pltpu.VMEM((n_slab, 64, 128), jnp.int16),
            pltpu.VMEM((n_slab, 64, 128), jnp.int16),
            pltpu.VMEM((n_slab // 2, 16, 128), BF16),
            pltpu.VMEM((n_slab, 16, 128), BF16),
            pltpu.VMEM((n_slab, 64, 256), F32),
            pltpu.VMEM((64, 256), BF16),
            pltpu.VMEM((2, 16, 256), BF16),
            pltpu.VMEM((2, 32, 256), BF16),
            pltpu.VMEM((6, 16, 256), BF16),
            pltpu.VMEM((4 * PITCH, 256), F32),
            pltpu.VMEM((24 * PITCH + 2 * PAD, 128), F32),
            pltpu.VMEM((24 * PITCH, 128), F32),
            pltpu.VMEM((22 * PITCH + 2 * PAD, 256), F32),
            pltpu.VMEM((20 * PITCH + 2 * PAD, 256), F32),
            pltpu.VMEM((18 * PITCH + 2 * PAD, 256), F32),
            pltpu.VMEM((22 * PITCH, 128), F32),
            pltpu.VMEM((384, 256), BF16),
            pltpu.VMEM((3, 1024, 256), BF16),
            pltpu.VMEM((256, 384), BF16),
            pltpu.VMEM((3, 17 * PITCH, 128), F32),
            pltpu.VMEM((3, 16, 256), F32),
            dma((n_tile,)),
            dma((n_tile,)),
            dma((n_tile,)),
            dma((n_tile,)),
            dma((n_slab,)),
            dma((n_slab,)),
            dma((n_slab,)),
            dma((n_slab,)),
            dma((8,)),
            dma((8,)),
        ],
        compiler_params=pltpu.CompilerParams(
            collective_id=0, has_side_effects=True, vmem_limit_bytes=62 * 1024 * 1024
        ),
    )(*operands)


def solution(mesh):
    return jax.shard_map(
        shards,
        mesh=mesh,
        in_specs=(
            P(("slab", "tile"), None),
            P(None, ("slab", "tile")),
            P(("slab", "tile")),
            P(("slab", "tile")),
            P(("slab", "tile")),
            P(None, "tile"),
            P(),
            P(),
            P(),
            P(),
            P(),
        ),
        out_specs=P(None, "slab", "tile"),
        check_vma=False,
    )
```
